256 devices in a mesh: wide: 32 (over z, x_lo, core), narrow: 8 (over x_hi, y).
Axes of the slice: x: 4 (x_hi: 2, x_lo: 2; x = x_hi * 2 + x_lo), y: 4, z: 8, core: 2. Of those that a mesh axis runs over, the one named last changes fastest.
Arguments:
- inputs: bfloat16 [768, 6144], P('wide', 'narrow'), may hold values from -60 to 60, as said below
- cotangent: bfloat16 [768, 6144], P('wide', 'narrow'), may hold values from -6 to 6
- norm_gain: float32 [6144], P('narrow'), may hold values from 0.25 to 1.75
- q_gain: float32 [128], replicated, may hold values from 0.5 to 2
- k_gain: float32 [128], replicated, may hold values from 0.5 to 2
- w_query: bfloat16 [6144, 4096], P('narrow', 'wide'), may hold values from -0.078125 to 0.078125
- w_key: bfloat16 [6144, 4096], P('narrow', 'wide'), may hold values from -0.078125 to 0.078125
- w_value: bfloat16 [6144, 4096], P('narrow', 'wide'), may hold values from -0.078125 to 0.078125
- w_out: bfloat16 [4096, 6144], P('wide', 'narrow'), may hold values from -0.09375 to 0.09375
- w_up: bfloat16 [6144, 24576], P('narrow', 'wide'), may hold values from -0.078125 to 0.078125
- w_down: bfloat16 [24576, 6144], P('wide', 'narrow'), may hold values from -0.0390625 to 0.0390625
Outputs:
- d_inputs: bfloat16 [768, 6144], P('wide', 'narrow')
- grad_query: bfloat16 [6144, 4096], P('narrow', 'wide')
- grad_key: bfloat16 [6144, 4096], P('narrow', 'wide')
- grad_value: bfloat16 [6144, 4096], P('narrow', 'wide')
- grad_out: bfloat16 [4096, 6144], P('wide', 'narrow')
- grad_up: bfloat16 [6144, 24576], P('narrow', 'wide')
- grad_down: bfloat16 [24576, 6144], P('wide', 'narrow')
- grad_norm_gain: float32 [6144], P('narrow')
- grad_qgain: float32 [128], replicated
- grad_kgain: float32 [128], replicated
The draws below stay inside these ranges and needn't reach their ends.
Inputs may be any that keep to these rules, and one draw needn't show every extreme that they name: `inputs`: activations entering the layer.
All inputs are finite; a program needn't handle non-finite values.
Results may differ from the reference program's by a relative error of at most 0.024.
Values may be sent and summed in bfloat16 or wider, within the bound.
A program may use at most 64 MiB of HBM per device.

```python
import math
import jax
import jax.numpy as jnp
from jax import lax

D = 6144
FF = 24576
HEADS = 32
HEAD_DIM = 128
PATCHES = 256
IMAGES = 3
TOKENS = 768


def draw_inputs(key, part):
    key = jax.random.fold_in(key, 11)
    key_cols = jax.random.fold_in(key, 1)
    key_rows = jax.random.fold_in(key, 2)
    key_body = jax.random.fold_in(key, 3)
    feature = jnp.arange(D, dtype=jnp.float32) / D
    column_scale = 0.1 * 10.0 ** (0.5 * feature + 0.5 * jax.random.uniform(key_cols, (D,), jnp.float32))
    row_scale = 10.0 ** jax.random.uniform(key_rows, (TOKENS, 1), jnp.float32)
    base = jnp.clip(jax.random.normal(key_body, (TOKENS, D), jnp.float32), -6.0, 6.0)
    return (base * column_scale * row_scale).astype(jnp.bfloat16)


def block_levels(key, dims, split, smallest, top_value):
    def one(dim, shards_of):
        steps = jax.random.uniform(jax.random.fold_in(jax.random.fold_in(key, 6), dim), (shards_of,), jnp.float32, smallest / len(split), top_value / len(split))
        return jnp.repeat(jnp.exp(steps), dims[dim] // shards_of).reshape((-1,) + (1,) * (len(dims) - dim - 1))

    gain = one(*split[0])
    for cut in split[1:]:
        gain = gain * one(*cut)
    return gain


def scatter_about(stream_key, dims, scale, bound, split=(), kind=jnp.bfloat16):
    drawn = jax.random.normal(stream_key, dims, jnp.float32) * scale
    if len(split) > 0:
        drawn = block_levels(stream_key, dims, split, -0.22, 0.18) * drawn
    return jnp.clip(drawn, min=-bound, max=bound).astype(kind)


def setup_inputs(seed: int = 0) -> dict:
    keys = jax.random.split(jax.random.key(seed), 12)
    inputs = draw_inputs(jax.random.fold_in(keys[11], 71), 0)
    cotangent = scatter_about(keys[1], (TOKENS, D), 1.0, 6.0, ((0, 32), (1, 8)))
    norm_gain = jnp.clip(1.0 + 0.15 * jax.random.normal(keys[2], (D,), jnp.float32), 0.25, 1.75)
    q_gain = jnp.clip(jnp.exp(jax.random.uniform(keys[3], (HEAD_DIM,), jnp.float32, math.log(0.5), math.log(2.0))), 0.5, 2.0)
    k_gain = jnp.clip(jnp.exp(jax.random.uniform(keys[4], (HEAD_DIM,), jnp.float32, math.log(0.5), math.log(2.0))), 0.5, 2.0)
    w_query = scatter_about(keys[5], (D, HEADS * HEAD_DIM), D ** -0.5, 0.078125, ((0, 8), (1, 32)))
    w_key = scatter_about(keys[6], (D, HEADS * HEAD_DIM), D ** -0.5, 0.078125, ((0, 8), (1, 32)))
    w_value = scatter_about(keys[7], (D, HEADS * HEAD_DIM), D ** -0.5, 0.078125, ((0, 8), (1, 32)))
    w_out = scatter_about(keys[8], (HEADS * HEAD_DIM, D), (HEADS * HEAD_DIM) ** -0.5, 0.09375, ((0, 32), (1, 8)))
    w_up = scatter_about(keys[9], (D, FF), D ** -0.5, 0.078125, ((0, 8), (1, 32)))
    w_down = scatter_about(keys[10], (FF, D), FF ** -0.5, 0.0390625, ((0, 32), (1, 8)))
    return dict(inputs=inputs, cotangent=cotangent, norm_gain=norm_gain, q_gain=q_gain, k_gain=k_gain, w_query=w_query, w_key=w_key, w_value=w_value, w_out=w_out, w_up=w_up, w_down=w_down)


epsilon = 1e-06

def head_norm(matrix):
    centre = lax.optimization_barrier(jnp.mean(matrix, axis=-1, keepdims=True))
    shifted = matrix - centre
    inv_std = lax.rsqrt(lax.optimization_barrier(jnp.mean(shifted * shifted, axis=-1, keepdims=True)) + epsilon)
    return (shifted * inv_std, inv_std)

def norm_back(upstream, normal, inv_std):
    first = lax.optimization_barrier(jnp.mean(upstream, axis=-1, keepdims=True))
    second = lax.optimization_barrier(jnp.mean(upstream * normal, axis=-1, keepdims=True))
    return inv_std * (upstream - first - normal * second)

def gelu_tanh(matrix):
    return jax.nn.gelu(matrix, approximate=True)

def product(left, right):
    return jnp.dot(left, right, preferred_element_type=jnp.float32)

def einsum_wide(form, left, right):
    return jnp.einsum(form, left.astype(jnp.float32), right.astype(jnp.float32), precision=lax.Precision.HIGHEST)

def reference(inputs, cotangent, norm_gain, q_gain, k_gain, w_query, w_key, w_value, w_out, w_up, w_down):
    as_float = inputs.astype(jnp.float32)
    row_mean = lax.optimization_barrier(jnp.mean(as_float, axis=1, keepdims=True))
    row_var = lax.optimization_barrier(jnp.mean(as_float * as_float, axis=1, keepdims=True)) - row_mean * row_mean
    row_rstd = lax.rsqrt(row_var + epsilon)
    unit_rows = (as_float - row_mean) * row_rstd
    normed = (unit_rows * norm_gain).astype(jnp.bfloat16)

    def split_heads(matrix):
        return matrix.reshape(IMAGES, PATCHES, HEADS, HEAD_DIM)
    q_unit, q_rstd = head_norm(split_heads(product(normed, w_query)))
    k_unit, k_rstd = head_norm(split_heads(product(normed, w_key)))
    values = split_heads(product(normed, w_value).astype(jnp.bfloat16))
    up_proj = product(normed, w_up)
    q_normed = (q_unit * q_gain).astype(jnp.bfloat16)
    k_normed = (k_unit * k_gain).astype(jnp.bfloat16)
    score_scale = HEAD_DIM ** (-0.5)
    scores = einsum_wide('iphd,iqhd->ihpq', q_normed, k_normed) * score_scale
    exponent = jnp.exp(scores)
    softmax_probs = exponent / lax.optimization_barrier(jnp.sum(exponent, axis=-1, keepdims=True))
    prob_low = softmax_probs.astype(jnp.bfloat16)
    attended = einsum_wide('ihpq,iqhd->iphd', prob_low, values).reshape(TOKENS, HEADS * HEAD_DIM).astype(jnp.bfloat16)
    gelu_out, gelu_pull = jax.vjp(gelu_tanh, up_proj)
    hidden = gelu_out.astype(jnp.bfloat16)
    d_att = product(cotangent, w_out.T).astype(jnp.bfloat16)
    d_hidden = product(cotangent, w_down.T)
    grad_out = product(attended.T, cotangent).astype(jnp.bfloat16)
    grad_down = product(hidden.T, cotangent).astype(jnp.bfloat16)
    d_up = gelu_pull(d_hidden)[0].astype(jnp.bfloat16)
    d_heads = split_heads(d_att)
    d_probs = einsum_wide('iphd,iqhd->ihpq', d_heads, values)
    d_values = einsum_wide('ihpq,iphd->iqhd', prob_low, d_heads).reshape(TOKENS, HEADS * HEAD_DIM).astype(jnp.bfloat16)
    d_scores = (softmax_probs * (d_probs - lax.optimization_barrier(jnp.sum(softmax_probs * d_probs, axis=-1, keepdims=True)))).astype(jnp.bfloat16)
    d_qnorm = einsum_wide('ihpq,iqhd->iphd', d_scores, k_normed) * score_scale
    d_knorm = einsum_wide('ihpq,iphd->iqhd', d_scores, q_normed) * score_scale
    grad_qgain = lax.optimization_barrier(jnp.sum(d_qnorm * q_unit, axis=(0, 1, 2)))
    grad_kgain = lax.optimization_barrier(jnp.sum(d_knorm * k_unit, axis=(0, 1, 2)))
    d_query = norm_back(d_qnorm * q_gain, q_unit, q_rstd).reshape(TOKENS, HEADS * HEAD_DIM).astype(jnp.bfloat16)
    d_key = norm_back(d_knorm * k_gain, k_unit, k_rstd).reshape(TOKENS, HEADS * HEAD_DIM).astype(jnp.bfloat16)
    grad_query = product(normed.T, d_query).astype(jnp.bfloat16)
    grad_key = product(normed.T, d_key).astype(jnp.bfloat16)
    grad_value = product(normed.T, d_values).astype(jnp.bfloat16)
    grad_up = product(normed.T, d_up).astype(jnp.bfloat16)
    d_normed = product(d_query, w_query.T) + product(d_key, w_key.T) + product(d_values, w_value.T) + product(d_up, w_up.T)
    grad_norm_gain = lax.optimization_barrier(jnp.sum(d_normed * unit_rows, axis=0))
    d_inputs = (cotangent.astype(jnp.float32) + norm_back(d_normed * norm_gain, unit_rows, row_rstd)).astype(jnp.bfloat16)
    return (d_inputs, grad_query, grad_key, grad_value, grad_out, grad_up, grad_down, grad_norm_gain, grad_qgain, grad_kgain)
```

```python
import functools
import math

import jax
import jax.numpy as jnp
from jax import lax
from jax.experimental import pallas as pl
from jax.experimental.pallas import tpu as pltpu
from jax.sharding import PartitionSpec as P

MESH = pl.DeviceIdType.MESH
F32 = jnp.float32
BF16 = jnp.bfloat16
EPS = 1e-06
PATCHES = 256
HEAD = 128
Z = 8
WIDE = 32
NARROW = 8
GELU_C = math.sqrt(2.0 / math.pi)
GELU_A = 0.044715


def nn(a, b):
    return lax.dot_general(a, b, (((1,), (0,)), ((), ())), preferred_element_type=F32)


def nt(a, b):
    return lax.dot_general(a, b, (((1,), (1,)), ((), ())), preferred_element_type=F32)


def tn(a, b):
    return lax.dot_general(a, b, (((0,), (0,)), ((), ())), preferred_element_type=F32)


def head_norm(matrix):
    centre = jnp.mean(matrix, axis=-1, keepdims=True)
    shifted = matrix - centre
    inv_std = lax.rsqrt(jnp.mean(shifted * shifted, axis=-1, keepdims=True) + EPS)
    return shifted * inv_std, inv_std


def norm_back(upstream, normal, inv_std):
    first = jnp.mean(upstream, axis=-1, keepdims=True)
    second = jnp.mean(upstream * normal, axis=-1, keepdims=True)
    return inv_std * (upstream - first - normal * second)


def gather_events():
    events = []
    for k in range(1, Z // 2):
        for d in range(2):
            for xs in range(2):
                events.append((2 + ((k - 1) * 2 + d) * 2 + xs, d, k, xs))
    return events


N_EVENTS = 2 + 4 * (Z // 2 - 1) + 2


def kernel(
    full_width,
    x_ref, cot_ref, ngain_ref, qgain_ref, kgain_ref,
    wq_hbm, wk_hbm, wv_hbm, wo_hbm, wu_hbm, wd_hbm,
    dx_ref, gq_ref, gk_ref, gv_ref, go_ref, gu_ref, gd_ref, gains_ref,
    wf, wdn,
    cg, ng, cf, nf,
    pd, pf, s1d, r1d, a1d, s2d, r2d, a2d, s3d, r3d,
    s1f, r1f, a1f, s2f, r2f, a2f, s3f, r3f,
    chunk_d, chunk_f,
    ga, gm, dqkv, att,
    dp, sc, rc, az, sz, rz, sx, rx,
    st, st2, gtile, gsib, gx, gz,
    wsem, ring_send, ring_recv, half_recv, sib_send, sib_recv, xp_send, xp_recv,
    rs_send, rs_recv, ag_send, ag_recv, st_send, st_recv,
    c_sem, z_send, z_recv, x_sem, g_sem, gz_send, gz_recv,
):
    w = lax.axis_index("wide")
    n = lax.axis_index("narrow")
    z = w // 4
    xl = (w // 2) % 2
    core = w % 2
    xh = n // 4
    y = n % 4
    zs = lambda k: (z + k + Z) % Z
    dev = lambda zz, xx, cc: zz * 4 + xx * 2 + cc

    bits = (((y + 1) // 2) % 2, y // 2, xh)
    cube = (
        (w, xh * 4 + y + 1 - 2 * (y % 2)),
        (w, xh * 4 + 3 - y),
        (w, (1 - xh) * 4 + y),
    )
    sibling = (dev(z, xl, 1 - core), n)
    xpartner = (dev(z, 1 - xl, core), n)
    z_next = ((dev(zs(1), xl, core), n), (dev(zs(-1), xl, core), n))
    z_peers = [(dev(zs(k), xl, core), n) for k in range(1, Z)]
    n_peers = [(w, (n + k) % NARROW) for k in range(1, NARROW)]

    pending = []

    def send(src, dst, ssem, rsem, to):
        copy = pltpu.make_async_remote_copy(
            src_ref=src, dst_ref=dst, send_sem=ssem, recv_sem=rsem, device_id=to, device_id_type=MESH
        )
        copy.start()
        pending.append(copy)
        return copy

    def recv(ref, ssem, rsem, frm):
        pltpu.make_async_remote_copy(
            src_ref=ref, dst_ref=ref, send_sem=ssem, recv_sem=rsem, device_id=frm, device_id_type=MESH
        ).wait_recv()

    wcopies = []
    for i, (src, dst) in enumerate((
        (wo_hbm, wdn.at[pl.ds(0, 128)]),
        (wd_hbm, wdn.at[pl.ds(128, 768)]),
        (wq_hbm, wf.at[:, pl.ds(0, 128)]),
        (wk_hbm, wf.at[:, pl.ds(128, 128)]),
        (wv_hbm, wf.at[:, pl.ds(256, 128)]),
        (wu_hbm, wf.at[:, pl.ds(384, 768)]),
    )):
        c = pltpu.make_async_copy(src, dst, wsem.at[i])
        c.start()
        wcopies.append(c)

    peers = [sibling, xpartner] + z_peers + n_peers
    barrier = pltpu.get_barrier_semaphore()
    for p in peers:
        pl.semaphore_signal(barrier, inc=1, device_id=p, device_id_type=MESH)
    pl.semaphore_wait(barrier, len(peers))

    half = cg.shape[-1] // 2

    def gather_own(g, i):
        slot = g.at[w]
        send(slot, slot, xp_send.at[i], xp_recv.at[i], xpartner)
        for d in range(2):
            send(slot, slot, ring_send.at[i, 0, d], ring_recv.at[i, 2 + d * 2], z_next[d])
        send(slot, slot, sib_send.at[i, 0], sib_recv.at[i, 0], sibling)

    def gather_partner(g, i):
        slot = g.at[dev(z, 1 - xl, core)]
        recv(slot, xp_send.at[i], xp_recv.at[i], xpartner)
        for d in range(2):
            send(slot, slot, ring_send.at[i, 1, d], ring_recv.at[i, 2 + d * 2 + 1], z_next[d])
        send(slot, slot, sib_send.at[i, 1], sib_recv.at[i, 1], sibling)

    def gather_step(g, i, k):
        for e, d, kk, xs in gather_events():
            if kk != k:
                continue
            x_at = xl if xs == 0 else 1 - xl
            slot = g.at[dev(zs(-k if d == 0 else k), x_at, core)]
            recv(slot, ring_send.at[i, e, d], ring_recv.at[i, e], z_next[1 - d])
            if k < Z // 2 - 1:
                send(slot, slot, ring_send.at[i, e, d], ring_recv.at[i, e + 4], z_next[d])
            else:
                part = slot.at[:, pl.ds(half * d, half)]
                send(part, part, ring_send.at[i, e, d], half_recv.at[i, d, xs], z_next[d])
            send(slot, slot, sib_send.at[i, e], sib_recv.at[i, e], sibling)

    def gather_far(g, i):
        for xs in range(2):
            x_at = xl if xs == 0 else 1 - xl
            slot = g.at[dev(zs(Z // 2), x_at, core)]
            e = N_EVENTS - 2 + xs
            for d in range(2):
                part = slot.at[:, pl.ds(half * d, half)]
                recv(part, ring_send.at[i, e, d], half_recv.at[i, d, xs], z_next[1 - d])
            send(slot, slot, sib_send.at[i, e], sib_recv.at[i, e], sibling)

    def gather_sibling(g, i):
        other = 1 - core
        recv(g.at[dev(z, xl, other)], sib_send.at[i, 0], sib_recv.at[i, 0], sibling)
        recv(g.at[dev(z, 1 - xl, other)], sib_send.at[i, 1], sib_recv.at[i, 1], sibling)
        for e, d, k, xs in gather_events():
            x_at = xl if xs == 0 else 1 - xl
            recv(g.at[dev(zs(-k if d == 0 else k), x_at, other)], sib_send.at[i, e], sib_recv.at[i, e], sibling)
        for xs in range(2):
            x_at = xl if xs == 0 else 1 - xl
            e = N_EVENTS - 2 + xs
            recv(g.at[dev(zs(Z // 2), x_at, other)], sib_send.at[i, e], sib_recv.at[i, e], sibling)

    def flatten(g, f):
        def body(p, _):
            both = jnp.concatenate([g[2 * p].astype(F32), g[2 * p + 1].astype(F32)], axis=0)
            f[pl.ds(pl.multiple_of(48 * p, 48), 48), :] = both.astype(BF16)
            return 0
        lax.fori_loop(0, WIDE // 2, body, 0)

    def small_sum(buf, j, a, b):
        lane = lax.broadcasted_iota(jnp.int32, (24, 128), 1)
        buf[n] = jnp.where(lane == 0, a, jnp.where(lane == 1, b, 0.0))
        for k, p in enumerate(n_peers):
            send(buf.at[n], buf.at[n], st_send.at[j, k], st_recv.at[j, k], p)

    def small_total(buf, j):
        for k in range(NARROW - 1):
            frm = (n - 1 - k + NARROW) % NARROW
            recv(buf.at[frm], st_send.at[j, k], st_recv.at[j, k], (w, frm))
        total = jnp.sum(buf[...], axis=0)
        return total[:, 0:1] / full_width, total[:, 1:2] / full_width

    cg[w] = cot_ref[...]
    gather_own(cg, 0)

    x = x_ref[...].astype(F32)
    small_sum(st, 0, jnp.sum(x, axis=1, keepdims=True), jnp.sum(x * x, axis=1, keepdims=True))
    gather_partner(cg, 0)
    row_mean, row_sq = small_total(st, 0)
    row_rstd = lax.rsqrt(row_sq - row_mean * row_mean + EPS)
    ng[w] = ((x_ref[...].astype(F32) - row_mean) * row_rstd * ngain_ref[...]).astype(BF16)
    gather_own(ng, 1)

    gather_step(cg, 0, 1)
    gather_partner(ng, 1)
    gather_step(cg, 0, 2)
    gather_step(ng, 1, 1)
    gather_step(cg, 0, 3)
    gather_step(ng, 1, 2)
    gather_far(cg, 0)
    gather_step(ng, 1, 3)
    gather_sibling(cg, 0)
    flatten(cg, cf)

    def at(ref, part, fixed):
        return ref.at[tuple(fixed.get(d, slice(None)) for d in range(3)) + (part,)]

    def rs_first(p, s1, r1, rnd):
        for r in range(3):
            s1[r] = at(p, r, {r: 1 - bits[r]})[...].astype(BF16)
            send(s1.at[r], r1.at[r], rs_send.at[rnd, 0, r], rs_recv.at[rnd, 0, r], cube[r])

    def rs_second(p, r1, a1, s2, r2, rnd):
        for r in range(3):
            e = (r + 1) % 3
            recv(r1.at[r], rs_send.at[rnd, 0, r], rs_recv.at[rnd, 0, r], cube[r])
            rest = [d for d in range(3) if d != r]
            pick = lambda v: tuple(v if d == e else slice(None) for d in rest)
            away, stay = 1 - bits[e], bits[e]
            s2[r] = (
                at(p, r, {r: bits[r], e: away})[...] + r1.at[(r,) + pick(away)][...].astype(F32)
            ).astype(BF16)
            send(s2.at[r], r2.at[r], rs_send.at[rnd, 1, r], rs_recv.at[rnd, 1, r], cube[e])
            a1[r] = at(p, r, {r: bits[r], e: stay})[...] + r1.at[(r,) + pick(stay)][...].astype(F32)

    def rs_third(r2, a1, s3, r3, a2, rnd):
        for r in range(3):
            e, f = (r + 1) % 3, (r + 2) % 3
            recv(r2.at[r], rs_send.at[rnd, 1, r], rs_recv.at[rnd, 1, r], cube[e])
            away, stay = 1 - bits[f], bits[f]
            s3[r] = (a1[r, away] + r2[r, away].astype(F32)).astype(BF16)
            send(s3.at[r], r3.at[r], rs_send.at[rnd, 2, r], rs_recv.at[rnd, 2, r], cube[f])
            a2[r] = a1[r, stay] + r2[r, stay].astype(F32)

    def rs_last(r3, a2, out, rnd):
        for r in range(3):
            f = (r + 2) % 3
            recv(r3.at[r], rs_send.at[rnd, 2, r], rs_recv.at[rnd, 2, r], cube[f])
            out[r] = a2[r] + r3[r].astype(F32)

    shape6 = lambda c: (2, 2, 2, 3, 32, c)

    wcopies[0].wait()
    wcopies[1].wait()
    pd[:, :, :, :, :, 0:128] = nt(cf[...], wdn[0:128, :]).reshape(shape6(128))
    for j in range(3):
        lo = 128 + 256 * j
        pd[:, :, :, :, :, lo:lo + 256] = nt(cf[...], wdn[lo:lo + 256, :]).reshape(shape6(256))
    rs_first(pd, s1d, r1d, 0)

    gather_far(ng, 1)
    gather_sibling(ng, 1)
    flatten(ng, nf)
    for c in wcopies[2:]:
        c.wait()
    for lo in range(0, 1152, 256):
        width = min(256, 1152 - lo)
        pf[:, :, :, :, :, lo:lo + width] = nn(nf[...], wf[:, lo:lo + width]).reshape(shape6(width))
    rs_first(pf, s1f, r1f, 1)

    rs_second(pd, r1d, a1d, s2d, r2d, 0)
    rs_second(pf, r1f, a1f, s2f, r2f, 1)
    rs_third(r2d, a1d, s3d, r3d, a2d, 0)
    rs_third(r2f, a1f, s3f, r3f, a2f, 1)
    rs_last(r3d, a2d, chunk_d, 0)
    rs_last(r3f, a2f, chunk_f, 1)

    def ag(buf, rnd, step):
        for r in range(3):
            order = ((r + 2) % 3, (r + 1) % 3, r)
            fixed = {d: bits[d] for d in order[step:]}
            src = at(buf, r, fixed)
            send(src, src, ag_send.at[rnd, step, r], ag_recv.at[rnd, step, r], cube[order[step]])

    def ag_wait(buf, rnd, step):
        for r in range(3):
            order = ((r + 2) % 3, (r + 1) % 3, r)
            fixed = {d: bits[d] for d in order[step:]}
            fixed[order[step]] = 1 - bits[order[step]]
            recv(at(buf, r, fixed), ag_send.at[rnd, step, r], ag_recv.at[rnd, step, r], cube[order[step]])

    mine = (bits[0], bits[1], bits[2])
    ga[mine + (slice(None), slice(None), pl.ds(0, 384))] = chunk_f[:, :, 0:384].astype(BF16)
    ga[mine + (slice(None), slice(None), pl.ds(384, 128))] = chunk_d[:, :, 0:128].astype(BF16)
    ag(ga, 0, 0)
    for r in range(3):
        up = chunk_f[r, :, 384:1152]
        dh = chunk_d[r, :, 128:896]
        sq = up * up
        t = jnp.tanh(GELU_C * up * (1.0 + GELU_A * sq))
        gm[mine + (r, slice(None), pl.ds(0, 768))] = (0.5 * up * (1.0 + t)).astype(BF16)
        slope = 0.5 * (1.0 + t) + 0.5 * up * (1.0 - t * t) * (GELU_C * (1.0 + 3.0 * GELU_A * sq))
        gm[mine + (r, slice(None), pl.ds(768, 768))] = (dh * slope).astype(BF16)
    ag(gm, 1, 0)
    ag_wait(ga, 0, 0)
    ag(ga, 0, 1)
    ag_wait(gm, 1, 0)
    ag(gm, 1, 1)
    ag_wait(ga, 0, 1)
    ag(ga, 0, 2)
    ag_wait(gm, 1, 1)
    ag(gm, 1, 2)
    ag_wait(ga, 0, 2)

    scale = HEAD ** (-0.5)
    qgain = qgain_ref[...]
    kgain = kgain_ref[...]
    qg = jnp.zeros((1, HEAD), F32)
    kg = jnp.zeros((1, HEAD), F32)
    for image in range(3):
        blocks = [(b // 3 // 4, b // 3 // 2 % 2, b // 3 % 2, b % 3) for b in range(image * 8, image * 8 + 8)]
        load = lambda lo: jnp.concatenate([ga[b + (slice(None), slice(lo, lo + 128))] for b in blocks], axis=0)
        q_unit, q_rstd = head_norm(load(0).astype(F32))
        k_unit, k_rstd = head_norm(load(128).astype(F32))
        values = load(256)
        d_att = load(384)
        q_normed = (q_unit * qgain).astype(BF16)
        k_normed = (k_unit * kgain).astype(BF16)
        exponent = jnp.exp(nt(q_normed, k_normed) * scale)
        probs = exponent / jnp.sum(exponent, axis=-1, keepdims=True)
        low = probs.astype(BF16)
        rows = slice(image * PATCHES, (image + 1) * PATCHES)
        att[rows, :] = nn(low, values).astype(BF16)
        d_probs = nt(d_att, values)
        dqkv[rows, 256:384] = tn(low, d_att).astype(BF16)
        d_scores = (probs * (d_probs - jnp.sum(probs * d_probs, axis=-1, keepdims=True))).astype(BF16)
        d_qnorm = nn(d_scores, k_normed) * scale
        d_knorm = tn(d_scores, q_normed) * scale
        qg = qg + jnp.sum(d_qnorm * q_unit, axis=0, keepdims=True)
        kg = kg + jnp.sum(d_knorm * k_unit, axis=0, keepdims=True)
        dqkv[rows, 0:128] = norm_back(d_qnorm * qgain, q_unit, q_rstd).astype(BF16)
        dqkv[rows, 128:256] = norm_back(d_knorm * kgain, k_unit, k_rstd).astype(BF16)

    go_ref[...] = tn(att[...], cf[...]).astype(BF16)
    for j in range(3):
        cols = slice(256 * j, 256 * j + 256)
        res = tn(nf[:, cols], dqkv[...]).astype(BF16)
        gq_ref[cols, :] = res[:, 0:128]
        gk_ref[cols, :] = res[:, 128:256]
        gv_ref[cols, :] = res[:, 256:384]

    ag_wait(gm, 1, 2)
    gain_rows = []
    for j in range(3):
        cols = slice(256 * j, 256 * j + 256)
        d_up = gm[:, :, :, :, :, 768:1536].reshape(768, 768)
        res = nt(dqkv[...], wf[cols, 0:384]) + nt(d_up, wf[cols, 384:1152])
        dp[:, :, :, :, cols] = res.reshape(Z, 2, 2, 24, 256)
        part = jnp.sum(res * nf[:, cols].astype(F32), axis=0, keepdims=True) / ngain_ref[:, cols]
        gain_rows += [part[:, 0:128], part[:, 128:256]]
    sc[...] = dp[:, :, pl.ds(1 - core, 1)].reshape(Z, 2, 24, 768).astype(BF16)
    core_copy = send(sc, rc, c_sem.at[0], c_sem.at[1], sibling)
    gtile[0] = jnp.concatenate(gain_rows + [qg, kg], axis=0)
    g_sib = send(gtile.at[0], gsib, g_sem.at[0], g_sem.at[1], sibling)

    core_copy.wait_recv()
    for k in range(1, Z):
        zz = zs(k)
        sz[k - 1] = (dp[zz, :, core] + rc[zz].astype(F32)).astype(BF16)
        send(sz.at[k - 1], rz.at[k - 1], z_send.at[k - 1], z_recv.at[k - 1], z_peers[k - 1])
    az[...] = dp[z, :, core] + rc[z].astype(F32)

    g_sib.wait_recv()
    gtile[1] = gtile[0] + gsib[...]
    g_xp = send(gtile.at[1], gx, g_sem.at[2], g_sem.at[3], xpartner)

    for j in range(3):
        cols = slice(256 * j, 256 * j + 256)
        d_up = gm[:, :, :, :, :, 768:1536].reshape(768, 768)
        gu_ref[cols, :] = tn(nf[:, cols], d_up).astype(BF16)
    g_xp.wait_recv()
    gtile[2] = gtile[1] + gx[...]
    for k in range(1, Z):
        send(gtile.at[2], gz.at[k - 1], gz_send.at[k - 1], gz_recv.at[k - 1], z_peers[k - 1])
    for j in range(3):
        cols = slice(256 * j, 256 * j + 256)
        hidden = gm[:, :, :, :, :, cols].reshape(768, 256)
        gd_ref[cols, :] = tn(hidden, cf[...]).astype(BF16)

    for k in range(1, Z):
        recv(rz.at[k - 1], z_send.at[k - 1], z_recv.at[k - 1], z_peers[Z - 1 - k])
        az[...] += rz[k - 1].astype(F32)
    sx[...] = az[1 - xl].astype(BF16)
    x_copy = send(sx, rx, x_sem.at[0], x_sem.at[1], xpartner)
    total = gtile[2]
    for k in range(1, Z):
        recv(gz.at[k - 1], gz_send.at[k - 1], gz_recv.at[k - 1], z_peers[Z - 1 - k])
        total = total + gz[k - 1]
    gains_ref[...] = total
    x_copy.wait_recv()
    d_unit = (az[xl] + rx[...].astype(F32)) * ngain_ref[...]
    unit = (x_ref[...].astype(F32) - row_mean) * row_rstd
    small_sum(st2, 1, jnp.sum(d_unit, axis=1, keepdims=True), jnp.sum(d_unit * unit, axis=1, keepdims=True))
    first, second = small_total(st2, 1)
    dx_ref[...] = (cot_ref[...].astype(F32) + row_rstd * (d_unit - first - unit * second)).astype(BF16)

    for c in pending:
        c.wait_send()


def per_device(inputs, cotangent, norm_gain, q_gain, k_gain, w_query, w_key, w_value, w_out, w_up, w_down):
    full_width = inputs.shape[1] * NARROW
    vm = pl.BlockSpec(memory_space=pltpu.VMEM)
    anywhere = pl.BlockSpec(memory_space=pl.ANY)
    v = pltpu.VMEM
    dma = pltpu.SemaphoreType.DMA

    def rs_buffers(c):
        return [
            v((3, 2, 2, 32, c), BF16), v((3, 2, 2, 32, c), BF16), v((3, 2, 32, c), F32),
            v((3, 2, 32, c), BF16), v((3, 2, 32, c), BF16), v((3, 32, c), F32),
            v((3, 32, c), BF16), v((3, 32, c), BF16),
        ]

    scratch = [
        v((768, 1152), BF16), v((896, 768), BF16),
        v((WIDE, 24, 768), BF16), v((WIDE, 24, 768), BF16), v((768, 768), BF16), v((768, 768), BF16),
        v((2, 2, 2, 3, 32, 896), F32), v((2, 2, 2, 3, 32, 1152), F32),
        *rs_buffers(896), *rs_buffers(1152),
        v((3, 32, 896), F32), v((3, 32, 1152), F32),
        v((2, 2, 2, 3, 32, 512), BF16), v((2, 2, 2, 3, 32, 1536), BF16), v((768, 384), BF16), v((768, 128), BF16),
        v((Z, 2, 2, 24, 768), F32), v((Z, 2, 24, 768), BF16), v((Z, 2, 24, 768), BF16), v((2, 24, 768), F32),
        v((Z - 1, 2, 24, 768), BF16), v((Z - 1, 2, 24, 768), BF16), v((24, 768), BF16), v((24, 768), BF16),
        v((NARROW, 24, 128), F32), v((NARROW, 24, 128), F32),
        v((3, 8, 128), F32), v((8, 128), F32), v((8, 128), F32), v((Z - 1, 8, 128), F32),
        dma((6,)), dma((2, N_EVENTS, 2)), dma((2, N_EVENTS)), dma((2, 2, 2)), dma((2, N_EVENTS)), dma((2, N_EVENTS)),
        dma((2,)), dma((2,)),
        dma((2, 3, 3)), dma((2, 3, 3)), dma((2, 3, 3)), dma((2, 3, 3)),
        dma((2, NARROW - 1)), dma((2, NARROW - 1)),
        dma((2,)), dma((Z - 1,)), dma((Z - 1,)), dma((2,)), dma((4,)), dma((Z - 1,)), dma((Z - 1,)),
    ]
    outs = pl.pallas_call(
        functools.partial(kernel, full_width),
        out_shape=(
            jax.ShapeDtypeStruct((24, 768), BF16),
            jax.ShapeDtypeStruct((768, 128), BF16),
            jax.ShapeDtypeStruct((768, 128), BF16),
            jax.ShapeDtypeStruct((768, 128), BF16),
            jax.ShapeDtypeStruct((128, 768), BF16),
            jax.ShapeDtypeStruct((768, 768), BF16),
            jax.ShapeDtypeStruct((768, 768), BF16),
            jax.ShapeDtypeStruct((8, 128), F32),
        ),
        in_specs=[vm] * 5 + [anywhere] * 6,
        out_specs=[vm] * 8,
        scratch_shapes=scratch,
        compiler_params=pltpu.CompilerParams(
            collective_id=0, has_side_effects=True, vmem_limit_bytes=60 * 1024 * 1024
        ),
    )(
        inputs, cotangent, norm_gain.reshape(1, -1), q_gain.reshape(1, -1), k_gain.reshape(1, -1),
        w_query, w_key, w_value, w_out, w_up, w_down,
    )
    gains = outs[7]
    return (*outs[:7], gains[:6].reshape(-1), gains[6], gains[7])


def solution(mesh):
    return jax.shard_map(
        per_device,
        mesh=mesh,
        in_specs=(
            P("wide", "narrow"), P("wide", "narrow"), P("narrow"), P(), P(),
            P("narrow", "wide"), P("narrow", "wide"), P("narrow", "wide"), P("wide", "narrow"),
            P("narrow", "wide"), P("wide", "narrow"),
        ),
        out_specs=(
            P("wide", "narrow"),
            P("narrow", "wide"), P("narrow", "wide"), P("narrow", "wide"), P("wide", "narrow"),
            P("narrow", "wide"), P("wide", "narrow"),
            P("narrow"), P(), P(),
        ),
        check_vma=False,
    )
```

```python
import functools
import math

import jax
import jax.numpy as jnp
from jax import lax
from jax.experimental import pallas as pl
from jax.experimental.pallas import tpu as pltpu
from jax.sharding import PartitionSpec as P

MESH = pl.DeviceIdType.MESH
F32 = jnp.float32
BF16 = jnp.bfloat16
EPS = 1e-06
PATCHES = 256
HEAD = 128
Z = 8
FAR = Z // 2
WIDE = 32
NARROW = 8
GELU_C = math.sqrt(2.0 / math.pi)
GELU_A = 0.044715


def nn(a, b):
    return lax.dot_general(a, b, (((1,), (0,)), ((), ())), preferred_element_type=F32)


def nt(a, b):
    return lax.dot_general(a, b, (((1,), (1,)), ((), ())), preferred_element_type=F32)


def tn(a, b):
    return lax.dot_general(a, b, (((0,), (0,)), ((), ())), preferred_element_type=F32)


def head_norm(matrix):
    centre = jnp.mean(matrix, axis=-1, keepdims=True)
    shifted = matrix - centre
    inv_std = lax.rsqrt(jnp.mean(shifted * shifted, axis=-1, keepdims=True) + EPS)
    return shifted * inv_std, inv_std


def norm_back(upstream, normal, inv_std):
    first = jnp.mean(upstream, axis=-1, keepdims=True)
    second = jnp.mean(upstream * normal, axis=-1, keepdims=True)
    return inv_std * (upstream - first - normal * second)


def kernel(
    full_width,
    x_ref, cot_ref, ngain_ref, qgain_ref, kgain_ref,
    wq_hbm, wk_hbm, wv_hbm, wo_hbm, wu_hbm, wd_hbm,
    dx, gq, gk, gv, go, gu, gd, gains,
    wf, wdn,
    cg, ng, cf, nf,
    pd, pq, pu,
    bde, bdl, bq, bul, bue,
    ga, gp, gh, dqkv, att,
    dp, sib_s, sib_r, x_s, x_r, z_s, z_r, fin, fin_s, fin_r,
    st, st2, gtile, gquad, gz,
    wsem, sib_send, sib_recv, xp_send, xp_recv, line_send, line_recv,
    rs_send, rs_recv, ag_send, ag_recv, st_send, st_recv,
    c_sem, x_sem, z_send, z_recv, f_sem, gq_send, gq_recv, gz_send, gz_recv,
):
    w = lax.axis_index("wide")
    n = lax.axis_index("narrow")
    z = w // 4
    xl = (w // 2) % 2
    core = w % 2
    xh = n // 4
    y = n % 4
    way = 1 - 2 * core
    zs = lambda k: (z + k + Z) % Z
    dev = lambda zz, xx, cc: zz * 4 + xx * 2 + cc

    bits = (((y + 1) // 2) % 2, y // 2, xh)
    cube = (
        (w, xh * 4 + y + 1 - 2 * (y % 2)),
        (w, xh * 4 + 3 - y),
        (w, (1 - xh) * 4 + y),
    )
    sibling = (dev(z, xl, 1 - core), n)
    quad = (sibling, (dev(z, 1 - xl, core), n), (dev(z, 1 - xl, 1 - core), n))
    quad_at = ((xl, 1 - core), (1 - xl, core), (1 - xl, 1 - core))
    xpartner = quad[1]
    z_peers = [(dev(zs(k), xl, core), n) for k in range(1, Z)]
    n_peers = [(w, (n + k) % NARROW) for k in range(1, NARROW)]

    pending = []

    def send(src, dst, ssem, rsem, to):
        copy = pltpu.make_async_remote_copy(
            src_ref=src, dst_ref=dst, send_sem=ssem, recv_sem=rsem, device_id=to, device_id_type=MESH
        )
        copy.start()
        pending.append(copy)

    def recv(ref, ssem, rsem, frm):
        pltpu.make_async_remote_copy(
            src_ref=ref, dst_ref=ref, send_sem=ssem, recv_sem=rsem, device_id=frm, device_id_type=MESH
        ).wait_recv()

    wcopies = []
    for i, (src, dst) in enumerate((
        (wo_hbm, wdn.at[pl.ds(0, 128)]),
        (wd_hbm, wdn.at[pl.ds(128, 768)]),
        (wq_hbm, wf.at[:, pl.ds(0, 128)]),
        (wk_hbm, wf.at[:, pl.ds(128, 128)]),
        (wv_hbm, wf.at[:, pl.ds(256, 128)]),
        (wu_hbm, wf.at[:, pl.ds(384, 768)]),
    )):
        c = pltpu.make_async_copy(src, dst, wsem.at[i])
        c.start()
        wcopies.append(c)

    peers = [*quad, *z_peers, *n_peers]
    barrier = pltpu.get_barrier_semaphore()
    for p in peers:
        pl.semaphore_signal(barrier, inc=1, device_id=p, device_id_type=MESH)
    ngain = jnp.concatenate([ngain_ref[pl.ds(128 * i, 128)].reshape(1, 128) for i in range(6)], axis=1)
    cg[z, xl, core] = cot_ref[...]
    pl.semaphore_wait(barrier, len(peers))

    def gather_own(g, i):
        slot = g.at[z, xl, core]
        send(slot, slot, sib_send.at[i, 0], sib_recv.at[i, 0], sibling)
        send(slot, slot, xp_send.at[i, 0], xp_recv.at[i, 0], xpartner)

    def gather_out(g, i):
        recv(g.at[z, xl, 1 - core], sib_send.at[i, 0], sib_recv.at[i, 0], sibling)
        for k in range(1, FAR + 1):
            slot = g.at[z, xl] if k < FAR else g.at[z, xl, core]
            send(slot, slot, line_send.at[i, k], line_recv.at[i, k], (dev(zs(way * k), xl, core), n))

    def gather_line(g, i, k):
        zz = zs(-way * k)
        slot = g.at[zz, xl] if k < FAR else g.at[zz, xl, core]
        recv(slot, line_send.at[i, k], line_recv.at[i, k], (dev(zz, xl, core), n))
        send(slot, slot, sib_send.at[i, k], sib_recv.at[i, k], sibling)
        send(slot, slot, xp_send.at[i, k], xp_recv.at[i, k], xpartner)

    def gather_x(g, i, k):
        zz = zs(-way * k)
        slot = g.at[zz, 1 - xl] if 0 < k < FAR else g.at[zz, 1 - xl, core]
        recv(slot, xp_send.at[i, k], xp_recv.at[i, k], xpartner)
        send(slot, slot, sib_send.at[i, FAR + 1 + k], sib_recv.at[i, FAR + 1 + k], sibling)

    def flatten(g, f, xx, zz):
        block = jnp.concatenate([g[zz, xx, 0].astype(F32), g[zz, xx, 1].astype(F32)], axis=0)
        f[xx, pl.ds(pl.multiple_of(48 * zz, 48), 48), :] = block.astype(BF16)

    def flatten_own(g, i, f, k):
        zz = zs(way * k)
        if k > 0:
            slot = g.at[zz, xl] if k < FAR else g.at[zz, xl, 1 - core]
            recv(slot, sib_send.at[i, k], sib_recv.at[i, k], sibling)
        flatten(g, f, xl, zz)
        if 0 < k < FAR:
            flatten(g, f, xl, zs(-way * k))

    def flatten_partner(g, i, f, k):
        zz = zs(way * k)
        slot = g.at[zz, 1 - xl] if 0 < k < FAR else g.at[zz, 1 - xl, 1 - core]
        recv(slot, sib_send.at[i, FAR + 1 + k], sib_recv.at[i, FAR + 1 + k], sibling)
        flatten(g, f, 1 - xl, zz)
        if 0 < k < FAR:
            flatten(g, f, 1 - xl, zs(-way * k))

    def small_sum(buf, j, a, b):
        lane = lax.broadcasted_iota(jnp.int32, (24, 128), 1)
        buf[n] = jnp.where(lane == 0, a, jnp.where(lane == 1, b, 0.0))
        for k, p in enumerate(n_peers):
            send(buf.at[n], buf.at[n], st_send.at[j, k], st_recv.at[j, k], p)

    def small_total(buf, j):
        for k in range(NARROW - 1):
            frm = (n - 1 - k + NARROW) % NARROW
            recv(buf.at[frm], st_send.at[j, k], st_recv.at[j, k], (w, frm))
        total = jnp.sum(buf[...], axis=0)
        return total[:, 0:1] / full_width, total[:, 1:2] / full_width

    gather_own(cg, 0)
    x = x_ref[...].astype(F32)
    small_sum(st, 0, jnp.sum(x, axis=1, keepdims=True), jnp.sum(x * x, axis=1, keepdims=True))
    gather_out(cg, 0)
    row_mean, row_sq = small_total(st, 0)
    row_rstd = lax.rsqrt(row_sq - row_mean * row_mean + EPS)
    ng[z, xl, core] = ((x_ref[...].astype(F32) - row_mean) * row_rstd * ngain).astype(BF16)
    gather_own(ng, 1)

    every = slice(None)

    def at(ref, half, part, fixed):
        return ref.at[(half,) + tuple(fixed.get(d, every) for d in range(3)) + (part,)]

    def lead(half):
        return (every,) if half is every else ()

    def rs_first(p, half, b, rnd):
        s1, r1 = b[0], b[1]
        for r in range(3):
            s1[r] = at(p, half, r, {r: 1 - bits[r]})[...].astype(BF16)
            send(s1.at[r], r1.at[r], rs_send.at[rnd, 0, r], rs_recv.at[rnd, 0, r], cube[r])

    def rs_second(p, half, b, rnd):
        r1, a1, s2, r2 = b[1:5]
        for r in range(3):
            e = (r + 1) % 3
            recv(r1.at[r], rs_send.at[rnd, 0, r], rs_recv.at[rnd, 0, r], cube[r])
            rest = [d for d in range(3) if d != r]
            pick = lambda v: (r,) + lead(half) + tuple(v if d == e else every for d in rest)
            away, stay = 1 - bits[e], bits[e]
            s2[r] = (
                at(p, half, r, {r: bits[r], e: away})[...] + r1.at[pick(away)][...].astype(F32)
            ).astype(BF16)
            send(s2.at[r], r2.at[r], rs_send.at[rnd, 1, r], rs_recv.at[rnd, 1, r], cube[e])
            a1[r] = at(p, half, r, {r: bits[r], e: stay})[...] + r1.at[pick(stay)][...].astype(F32)

    def rs_third(half, b, rnd):
        a1, r2, a2, s3, r3 = b[2], b[4], b[5], b[6], b[7]
        for r in range(3):
            e, f = (r + 1) % 3, (r + 2) % 3
            recv(r2.at[r], rs_send.at[rnd, 1, r], rs_recv.at[rnd, 1, r], cube[e])
            away, stay = (r,) + lead(half) + (1 - bits[f],), (r,) + lead(half) + (bits[f],)
            s3[r] = (a1[away] + r2[away].astype(F32)).astype(BF16)
            send(s3.at[r], r3.at[r], rs_send.at[rnd, 2, r], rs_recv.at[rnd, 2, r], cube[f])
            a2[r] = a1[stay] + r2[stay].astype(F32)

    def rs_last(b, rnd):
        a2, r3 = b[5], b[7]
        for r in range(3):
            f = (r + 2) % 3
            recv(r3.at[r], rs_send.at[rnd, 2, r], rs_recv.at[rnd, 2, r], cube[f])
            a2[r] = a2[r] + r3[r].astype(F32)

    def cot_products(half):
        lhs = lambda: cf[half]
        shape = lambda c: (2, 2, 2, 3, 16, c)
        pd[half, :, :, :, :, :, 0:128] = nt(lhs(), wdn[0:128, :]).reshape(shape(128))
        for j in range(3):
            lo = 128 + 256 * j
            pd[half, :, :, :, :, :, lo:lo + 256] = nt(lhs(), wdn[lo:lo + 256, :]).reshape(shape(256))

    def ag(buf, half, rnd, step):
        for r in range(3):
            order = ((r + 2) % 3, (r + 1) % 3, r)
            src = at(buf, half, r, {d: bits[d] for d in order[step:]})
            send(src, src, ag_send.at[rnd, step, r], ag_recv.at[rnd, step, r], cube[order[step]])

    def ag_wait(buf, half, rnd, step):
        for r in range(3):
            order = ((r + 2) % 3, (r + 1) % 3, r)
            fixed = {d: bits[d] for d in order[step:]}
            fixed[order[step]] = 1 - bits[order[step]]
            recv(
                at(buf, half, r, fixed), ag_send.at[rnd, step, r], ag_recv.at[rnd, step, r], cube[order[step]]
            )

    mine = (bits[0], bits[1], bits[2])
    theirs = 1 - xl

    def gelu(half, b_up, b_d):
        up = b_up[5][...]
        sq = up * up
        t = jnp.tanh(GELU_C * up * (1.0 + GELU_A * sq))
        gh[(half,) + mine] = (0.5 * up * (1.0 + t)).astype(BF16)
        slope = 0.5 * (1.0 + t) + 0.5 * up * (1.0 - t * t) * (GELU_C * (1.0 + 3.0 * GELU_A * sq))
        gp[(half,) + mine] = (b_d[5][:, :, 128:896] * slope).astype(BF16)

    gather_line(cg, 0, 1)
    gather_line(cg, 0, 2)
    gather_out(ng, 1)
    gather_x(cg, 0, 0)
    gather_line(cg, 0, 3)
    gather_x(cg, 0, 1)
    gather_line(cg, 0, 4)
    flatten_own(cg, 0, cf, 0)
    flatten_own(cg, 0, cf, 1)
    gather_x(cg, 0, 2)
    flatten_own(cg, 0, cf, 2)
    flatten_own(cg, 0, cf, 3)
    flatten_own(cg, 0, cf, 4)
    wcopies[0].wait()
    wcopies[1].wait()
    cot_products(xl)
    rs_first(pd, xl, bde, 0)

    gather_x(cg, 0, 3)
    gather_line(ng, 1, 1)
    gather_x(cg, 0, 4)
    gather_line(ng, 1, 2)
    gather_x(ng, 1, 0)
    for k in range(FAR + 1):
        flatten_partner(cg, 0, cf, k)
    gather_line(ng, 1, 3)
    gather_x(ng, 1, 1)
    gather_line(ng, 1, 4)
    cot_products(theirs)
    rs_first(pd, theirs, bdl, 1)

    gather_x(ng, 1, 2)
    flatten_own(ng, 1, nf, 0)
    flatten_own(ng, 1, nf, 1)
    flatten_own(ng, 1, nf, 2)
    gather_x(ng, 1, 3)
    flatten_own(ng, 1, nf, 3)
    flatten_own(ng, 1, nf, 4)
    gather_x(ng, 1, 4)
    rs_second(pd, xl, bde, 0)
    for k in range(FAR + 1):
        flatten_partner(ng, 1, nf, k)
    for c in wcopies[2:]:
        c.wait()
    lhs = lambda: nf[...].reshape(768, 768)
    shape = lambda c: (2, 2, 2, 2, 3, 16, c)
    pq[:, :, :, :, :, :, 0:256] = nn(lhs(), wf[:, 0:256]).reshape(shape(256))
    pq[:, :, :, :, :, :, 256:384] = nn(lhs(), wf[:, 256:384]).reshape(shape(128))
    rs_first(pq, every, bq, 2)
    rs_second(pd, theirs, bdl, 1)
    for j in range(3):
        lo = 256 * j
        pu[:, :, :, :, :, :, lo:lo + 256] = nn(lhs(), wf[:, 384 + lo:640 + lo]).reshape(shape(256))
    rs_first(pu, theirs, bul, 3)
    rs_first(pu, xl, bue, 4)

    rs_third(xl, bde, 0)
    rs_second(pq, every, bq, 2)
    rs_third(theirs, bdl, 1)
    rs_second(pu, theirs, bul, 3)
    rs_last(bde, 0)
    rs_third(every, bq, 2)
    rs_last(bdl, 1)
    rs_second(pu, xl, bue, 4)
    rs_last(bq, 2)
    for r in range(3):
        ga[(every,) + mine + (r, every, pl.ds(0, 384))] = bq[5][r].astype(BF16)
    ga[(xl,) + mine + (every, every, pl.ds(384, 128))] = bde[5][:, :, 0:128].astype(BF16)
    ga[(theirs,) + mine + (every, every, pl.ds(384, 128))] = bdl[5][:, :, 0:128].astype(BF16)
    ag(ga, every, 0, 0)
    rs_third(theirs, bul, 3)
    rs_third(xl, bue, 4)
    ag_wait(ga, every, 0, 0)
    ag(ga, every, 0, 1)
    rs_last(bul, 3)
    gelu(theirs, bul, bdl)
    ag(gp, theirs, 1, 0)
    rs_last(bue, 4)
    gelu(xl, bue, bde)
    ag(gp, xl, 2, 0)
    ag_wait(ga, every, 0, 1)
    ag(ga, every, 0, 2)
    ag_wait(gp, theirs, 1, 0)
    ag(gp, theirs, 1, 1)
    ag(gh, every, 3, 0)
    ag_wait(gp, xl, 2, 0)
    ag(gp, xl, 2, 1)
    ag_wait(ga, every, 0, 2)

    scale = HEAD ** (-0.5)
    qgain = qgain_ref[...]
    kgain = kgain_ref[...]
    gain_sums = [jnp.zeros((1, HEAD), F32), jnp.zeros((1, HEAD), F32)]

    def attention(image):
        places = [(b % 6 // 3, b // 6, b % 3) for b in range(image * 16, image * 16 + 16)]
        load = lambda lo: jnp.concatenate(
            [ga[xx, c // 4, c // 2 % 2, c % 2, r, :, lo:lo + 128] for xx, c, r in places], axis=0
        )

        def store(ref, lo, value):
            for i, (xx, c, r) in enumerate(places):
                ref[xx, c, r, :, lo:lo + 128] = value[16 * i:16 * i + 16]

        q_unit, q_rstd = head_norm(load(0).astype(F32))
        k_unit, k_rstd = head_norm(load(128).astype(F32))
        values = load(256)
        d_att = load(384)
        q_normed = (q_unit * qgain).astype(BF16)
        k_normed = (k_unit * kgain).astype(BF16)
        exponent = jnp.exp(nt(q_normed, k_normed) * scale)
        probs = exponent / jnp.sum(exponent, axis=-1, keepdims=True)
        low = probs.astype(BF16)
        store(att, 0, nn(low, values).astype(BF16))
        d_probs = nt(d_att, values)
        store(dqkv, 256, tn(low, d_att).astype(BF16))
        d_scores = (probs * (d_probs - jnp.sum(probs * d_probs, axis=-1, keepdims=True))).astype(BF16)
        d_qnorm = nn(d_scores, k_normed) * scale
        d_knorm = tn(d_scores, q_normed) * scale
        gain_sums[0] = gain_sums[0] + jnp.sum(d_qnorm * q_unit, axis=0, keepdims=True)
        gain_sums[1] = gain_sums[1] + jnp.sum(d_knorm * k_unit, axis=0, keepdims=True)
        store(dqkv, 0, norm_back(d_qnorm * qgain, q_unit, q_rstd).astype(BF16))
        store(dqkv, 128, norm_back(d_knorm * kgain, k_unit, k_rstd).astype(BF16))

    attention(0)
    ag_wait(gp, theirs, 1, 1)
    ag(gp, theirs, 1, 2)
    ag_wait(gh, every, 3, 0)
    ag(gh, every, 3, 1)
    attention(1)
    ag_wait(gp, xl, 2, 1)
    ag(gp, xl, 2, 2)
    attention(2)

    gain_rows = []

    def products(half, e):
        d_heads = lambda: dqkv[half].reshape(384, 384)
        d_up = lambda: gp[half].reshape(384, 768)
        for j in range(3):
            cols = slice(256 * j, 256 * j + 256)
            res = nt(d_heads(), wf[cols, 0:384]) + nt(d_up(), wf[cols, 384:1152])
            dp[e, :, :, :, cols] = res.reshape(Z, 2, 24, 256)
            part = jnp.sum(res * nf[half, :, cols].astype(F32), axis=0, keepdims=True) / ngain[:, cols]
            gain_rows.append(part)
        for k in range(1, FAR):
            sib_s[e, k - 1] = dp[e, zs(-way * k)].astype(BF16)
        sib_s[e, FAR - 1, 0] = dp[e, zs(FAR), 1 - core].astype(BF16)
        sib_s[e, FAR - 1, 1] = dp[e, z, 1 - core].astype(BF16)
        send(sib_s.at[e], sib_r.at[e], c_sem.at[e, 0], c_sem.at[e, 1], sibling)

    def pair(e, k):
        return dp[e, zs(way * k)] + sib_r[e, k - 1].astype(F32)

    def far(e):
        return dp[e, zs(FAR), core] + sib_r[e, FAR - 1, 0].astype(F32)

    def near(e):
        return dp[e, z, core] + sib_r[e, FAR - 1, 1].astype(F32)

    ag_wait(gp, theirs, 1, 2)
    products(theirs, 0)
    ag_wait(gh, every, 3, 1)
    recv(sib_r.at[0], c_sem.at[0, 0], c_sem.at[0, 1], sibling)
    for k in range(1, FAR):
        x_s[k - 1] = pair(0, k).astype(BF16)
    x_s[FAR - 1, 0] = far(0).astype(BF16)
    x_s[FAR - 1, 1] = near(0).astype(BF16)
    send(x_s, x_r, x_sem.at[0], x_sem.at[1], xpartner)

    ag_wait(gp, xl, 2, 2)
    ag(gh, every, 3, 2)
    products(xl, 1)
    gain_rows = [
        (gain_rows[j] + gain_rows[j + 3])[:, 128 * i:128 * i + 128] for j in range(3) for i in range(2)
    ]
    gtile[0] = jnp.concatenate(gain_rows + gain_sums, axis=0)
    for j in range(3):
        send(gtile.at[0], gquad.at[j], gq_send.at[j], gq_recv.at[j], quad[j])
    recv(x_r, x_sem.at[0], x_sem.at[1], xpartner)
    recv(sib_r.at[1], c_sem.at[1, 0], c_sem.at[1, 1], sibling)
    for k in range(FAR - 1, 0, -1):
        z_s[k - 1] = (pair(1, k) + x_r[k - 1].astype(F32)).astype(BF16)
        send(z_s.at[k - 1], z_r.at[k - 1], z_send.at[k], z_recv.at[k], (dev(zs(way * k), xl, core), n))
    z_s[FAR - 1, 0] = (far(1) + x_r[FAR - 1, 0].astype(F32)).astype(BF16)
    send(
        z_s.at[FAR - 1, 0], z_r.at[FAR - 1, 0], z_send.at[FAR], z_recv.at[FAR], (dev(zs(FAR), xl, core), n)
    )
    fin[core] = near(1) + x_r[FAR - 1, 1].astype(F32)
    for j in range(3):
        recv(gquad.at[j], gq_send.at[j], gq_recv.at[j], quad[j])
    gtile[1] = gtile[0] + gquad[0] + gquad[1] + gquad[2]
    for k in range(1, Z):
        send(gtile.at[1], gz.at[k - 1], gz_send.at[k - 1], gz_recv.at[k - 1], z_peers[k - 1])

    for j in range(3):
        cols = slice(256 * j, 256 * j + 256)
        left = nf[:, :, cols].reshape(768, 256)
        gu[cols, :] = tn(left, gp[...].reshape(768, 768)).astype(BF16)
        res = tn(left, dqkv[...].reshape(768, 384)).astype(BF16)
        gq[cols, :] = res[:, 0:128]
        gk[cols, :] = res[:, 128:256]
        gv[cols, :] = res[:, 256:384]

    recv(z_r.at[FAR - 1, 0], z_send.at[FAR], z_recv.at[FAR], (dev(zs(FAR), xl, core), n))
    for k in range(1, FAR):
        recv(z_r.at[k - 1], z_send.at[k], z_recv.at[k], (dev(zs(-way * k), xl, core), n))
    fin[1 - core] = sum(z_r[k, 1 - core].astype(F32) for k in range(FAR - 1))
    fin_s[...] = fin[1 - core].astype(BF16)
    send(fin_s, fin_r, f_sem.at[0], f_sem.at[1], sibling)

    go[...] = tn(att[...].reshape(768, 128), cf[...].reshape(768, 768)).astype(BF16)

    d_own = fin[core] + z_r[FAR - 1, 0].astype(F32) + sum(z_r[k, core].astype(F32) for k in range(FAR - 1))
    recv(fin_r, f_sem.at[0], f_sem.at[1], sibling)
    d_normed = d_own + fin_r[...].astype(F32)
    d_unit = d_normed * ngain
    unit = (x_ref[...].astype(F32) - row_mean) * row_rstd
    small_sum(st2, 1, jnp.sum(d_unit, axis=1, keepdims=True), jnp.sum(d_unit * unit, axis=1, keepdims=True))

    ag_wait(gh, every, 3, 2)
    for j in range(3):
        cols = slice(256 * j, 256 * j + 256)
        hidden = gh[:, :, :, :, :, :, cols].reshape(768, 256)
        gd[cols, :] = tn(hidden, cf[...].reshape(768, 768)).astype(BF16)
    total = gtile[1]
    for k in range(1, Z):
        recv(gz.at[k - 1], gz_send.at[k - 1], gz_recv.at[k - 1], z_peers[Z - 1 - k])
        total = total + gz[k - 1]
    gains[...] = total

    first, second = small_total(st2, 1)
    dx[...] = (cot_ref[...].astype(F32) + row_rstd * (d_unit - first - unit * second)).astype(BF16)

    for c in pending:
        c.wait_send()


def hand_over(*refs):
    srcs, gains_ref, outs, (ngain_ref, qg_ref, kg_ref), sem = refs[:7], refs[7], refs[8:15], refs[15:18], refs[18]
    copies = [pltpu.make_async_copy(s, o, sem.at[i]) for i, (s, o) in enumerate(zip(srcs, outs))]
    for c in copies:
        c.start()
    for i in range(6):
        ngain_ref[pl.ds(128 * i, 128)] = gains_ref[i, :]
    qg_ref[...] = gains_ref[6, :]
    kg_ref[...] = gains_ref[7, :]
    for c in copies:
        c.wait()


def per_device(inputs, cotangent, norm_gain, q_gain, k_gain, w_query, w_key, w_value, w_out, w_up, w_down):
    full_width = inputs.shape[1] * NARROW
    vm = pl.BlockSpec(memory_space=pltpu.VMEM)
    anywhere = pl.BlockSpec(memory_space=pl.ANY)
    v = pltpu.VMEM
    dma = pltpu.SemaphoreType.DMA

    def rs_buffers(c, lead=()):
        return [
            v((3, *lead, 2, 2, 16, c), BF16), v((3, *lead, 2, 2, 16, c), BF16), v((3, *lead, 2, 16, c), F32),
            v((3, *lead, 2, 16, c), BF16), v((3, *lead, 2, 16, c), BF16), v((3, *lead, 16, c), F32),
            v((3, *lead, 16, c), BF16), v((3, *lead, 16, c), BF16),
        ]

    grads = [(24, 768), (768, 128), (768, 128), (768, 128), (128, 768), (768, 768), (768, 768)]
    cube = (2, 2, 2, 2, 3, 16)
    scratch = [
        v((768, 1152), BF16), v((896, 768), BF16),
        v((Z, 2, 2, 24, 768), BF16), v((Z, 2, 2, 24, 768), BF16), v((2, 384, 768), BF16), v((2, 384, 768), BF16),
        v((*cube, 896), F32), v((*cube, 384), F32), v((*cube, 768), F32),
        rs_buffers(896), rs_buffers(896), rs_buffers(384, (2,)), rs_buffers(768), rs_buffers(768),
        v((*cube, 512), BF16), v((*cube, 768), BF16), v((*cube, 768), BF16),
        v((2, 8, 3, 16, 384), BF16), v((2, 8, 3, 16, 128), BF16),
        v((2, Z, 2, 24, 768), F32), v((2, 4, 2, 24, 768), BF16), v((2, 4, 2, 24, 768), BF16),
        v((4, 2, 24, 768), BF16), v((4, 2, 24, 768), BF16), v((4, 2, 24, 768), BF16), v((4, 2, 24, 768), BF16),
        v((2, 24, 768), F32), v((24, 768), BF16), v((24, 768), BF16),
        v((NARROW, 24, 128), F32), v((NARROW, 24, 128), F32),
        v((2, 8, 128), F32), v((3, 8, 128), F32), v((Z - 1, 8, 128), F32),
        dma((6,)), dma((2, 10)), dma((2, 10)), dma((2, 5)), dma((2, 5)), dma((2, 5)), dma((2, 5)),
        dma((5, 3, 3)), dma((5, 3, 3)), dma((4, 3, 3)), dma((4, 3, 3)),
        dma((2, NARROW - 1)), dma((2, NARROW - 1)),
        dma((2, 2)), dma((2,)), dma((5,)), dma((5,)), dma((2,)), dma((3,)), dma((3,)),
        dma((Z - 1,)), dma((Z - 1,)),
    ]
    grad_shapes = [jax.ShapeDtypeStruct(g, BF16) for g in grads]
    outs = pl.pallas_call(
        functools.partial(kernel, full_width),
        out_shape=(*[v(g, BF16) for g in grads], v((8, 128), F32)),
        in_specs=[vm] * 5 + [pl.BlockSpec(memory_space=pltpu.HBM)] * 6,
        out_specs=[vm] * 8,
        scratch_shapes=scratch,
        compiler_params=pltpu.CompilerParams(
            collective_id=0, has_side_effects=True, vmem_limit_bytes=56 * 1024 * 1024
        ),
        name="layer",
    )(
        inputs, cotangent, norm_gain, q_gain.reshape(1, -1), k_gain.reshape(1, -1),
        w_query, w_key, w_value, w_out, w_up, w_down,
    )
    return pl.pallas_call(
        hand_over,
        out_shape=(
            *grad_shapes,
            jax.ShapeDtypeStruct((768,), F32), jax.ShapeDtypeStruct((128,), F32), jax.ShapeDtypeStruct((128,), F32),
        ),
        in_specs=[vm] * 8,
        out_specs=[anywhere] * 7 + [vm] * 3,
        scratch_shapes=[dma((7,))],
        name="hand_over",
    )(*[pltpu.with_memory_space_constraint(o, pltpu.VMEM) for o in outs])


def solution(mesh):
    return jax.shard_map(
        per_device,
        mesh=mesh,
        in_specs=(
            P("wide", "narrow"), P("wide", "narrow"), P("narrow"), P(), P(),
            P("narrow", "wide"), P("narrow", "wide"), P("narrow", "wide"), P("wide", "narrow"),
            P("narrow", "wide"), P("wide", "narrow"),
        ),
        out_specs=(
            P("wide", "narrow"),
            P("narrow", "wide"), P("narrow", "wide"), P("narrow", "wide"), P("wide", "narrow"),
            P("narrow", "wide"), P("wide", "narrow"),
            P("narrow"), P(), P(),
        ),
        check_vma=False,
    )
```

```python
import functools
import math

import jax
import jax.numpy as jnp
from jax import lax
from jax.experimental import pallas as pl
from jax.experimental.pallas import tpu as pltpu
from jax.sharding import PartitionSpec as P

MESH = pl.DeviceIdType.MESH
F32 = jnp.float32
BF16 = jnp.bfloat16
EPS = 1e-06
PATCHES = 256
HEAD = 128
Z = 8
FAR = Z // 2
WIDE = 32
NARROW = 8
GELU_C = math.sqrt(2.0 / math.pi)
GELU_A = 0.044715


def nn(a, b):
    return lax.dot_general(a, b, (((1,), (0,)), ((), ())), preferred_element_type=F32)


def nt(a, b):
    return lax.dot_general(a, b, (((1,), (1,)), ((), ())), preferred_element_type=F32)


def tn(a, b):
    return lax.dot_general(a, b, (((0,), (0,)), ((), ())), preferred_element_type=F32)


def head_norm(matrix):
    centre = jnp.mean(matrix, axis=-1, keepdims=True)
    shifted = matrix - centre
    inv_std = lax.rsqrt(jnp.mean(shifted * shifted, axis=-1, keepdims=True) + EPS)
    return shifted * inv_std, inv_std


def norm_back(upstream, normal, inv_std):
    first = jnp.mean(upstream, axis=-1, keepdims=True)
    second = jnp.mean(upstream * normal, axis=-1, keepdims=True)
    return inv_std * (upstream - first - normal * second)


def kernel(
    full_width,
    x_ref, cot_ref, ngain_ref, qgain_ref, kgain_ref,
    wq_hbm, wk_hbm, wv_hbm, wo_hbm, wu_hbm, wd_hbm,
    dx, gq, gk, gv, go, gu, gd, gains,
    wf, wdn,
    cg, ng, cf, nf,
    pd, pq, pu,
    bde, bdl, bqe, bql, bul, bue,
    ga, gp, gh, dqkv, att,
    dp, sib_s, sib_r, x_s, x_r, z_s, z_r, fin, fin_s, fin_r,
    st, rows, tile, gquad, gz,
    wsem, sib_send, sib_recv, xp_send, xp_recv, line_send, line_recv,
    rs_send, rs_recv, ag_send, ag_recv, st_send, st_recv,
    c_send, c_recv, x_send, x_recv, z_send, z_recv, f_sem, gq_send, gq_recv, gz_send, gz_recv,
):
    w = lax.axis_index("wide")
    n = lax.axis_index("narrow")
    z = w // 4
    xl = (w // 2) % 2
    core = w % 2
    xh = n // 4
    y = n % 4
    way = 1 - 2 * core
    zs = lambda k: (z + k + Z) % Z
    dev = lambda zz, xx, cc: zz * 4 + xx * 2 + cc

    bits = (((y + 1) // 2) % 2, y // 2, xh)
    cube = (
        (w, xh * 4 + y + 1 - 2 * (y % 2)),
        (w, xh * 4 + 3 - y),
        (w, (1 - xh) * 4 + y),
    )
    sibling = (dev(z, xl, 1 - core), n)
    quad = (sibling, (dev(z, 1 - xl, core), n), (dev(z, 1 - xl, 1 - core), n))
    quad_at = ((xl, 1 - core), (1 - xl, core), (1 - xl, 1 - core))
    xpartner = quad[1]
    z_peers = [(dev(zs(k), xl, core), n) for k in range(1, Z)]
    n_peers = [(w, (n + k) % NARROW) for k in range(1, NARROW)]

    pending = []

    def send(src, dst, ssem, rsem, to):
        copy = pltpu.make_async_remote_copy(
            src_ref=src, dst_ref=dst, send_sem=ssem, recv_sem=rsem, device_id=to, device_id_type=MESH
        )
        copy.start()
        pending.append(copy)

    def recv(ref, ssem, rsem, frm):
        pltpu.make_async_remote_copy(
            src_ref=ref, dst_ref=ref, send_sem=ssem, recv_sem=rsem, device_id=frm, device_id_type=MESH
        ).wait_recv()

    wcopies = []
    for i, (src, dst) in enumerate((
        (wo_hbm, wdn.at[pl.ds(0, 128)]),
        (wd_hbm, wdn.at[pl.ds(128, 768)]),
        (wq_hbm, wf.at[:, pl.ds(0, 128)]),
        (wk_hbm, wf.at[:, pl.ds(128, 128)]),
        (wv_hbm, wf.at[:, pl.ds(256, 128)]),
        (wu_hbm, wf.at[:, pl.ds(384, 768)]),
    )):
        c = pltpu.make_async_copy(src, dst, wsem.at[i])
        c.start()
        wcopies.append(c)

    peers = [*quad, *z_peers, *n_peers]
    barrier = pltpu.get_barrier_semaphore()
    for p in peers:
        pl.semaphore_signal(barrier, inc=1, device_id=p, device_id_type=MESH)
    ngain = jnp.concatenate([ngain_ref[pl.ds(128 * i, 128)].reshape(1, 128) for i in range(6)], axis=1)
    cg[z, xl, core] = cot_ref[...]
    pl.semaphore_wait(barrier, len(peers))

    def gather_own(g, i):
        slot = g.at[z, xl, core]
        send(slot, slot, sib_send.at[i, 0], sib_recv.at[i, 0], sibling)
        send(slot, slot, xp_send.at[i, 0], xp_recv.at[i, 0], xpartner)

    def gather_out(g, i):
        recv(g.at[z, xl, 1 - core], sib_send.at[i, 0], sib_recv.at[i, 0], sibling)
        for k in range(1, FAR + 1):
            slot = g.at[z, xl] if k < FAR else g.at[z, xl, core]
            send(slot, slot, line_send.at[i, k], line_recv.at[i, k], (dev(zs(way * k), xl, core), n))

    def gather_line(g, i, k):
        zz = zs(-way * k)
        slot = g.at[zz, xl] if k < FAR else g.at[zz, xl, core]
        recv(slot, line_send.at[i, k], line_recv.at[i, k], (dev(zz, xl, core), n))
        send(slot, slot, sib_send.at[i, k], sib_recv.at[i, k], sibling)
        send(slot, slot, xp_send.at[i, k], xp_recv.at[i, k], xpartner)

    def gather_x(g, i, k):
        zz = zs(-way * k)
        slot = g.at[zz, 1 - xl] if 0 < k < FAR else g.at[zz, 1 - xl, core]
        recv(slot, xp_send.at[i, k], xp_recv.at[i, k], xpartner)
        send(slot, slot, sib_send.at[i, FAR + 1 + k], sib_recv.at[i, FAR + 1 + k], sibling)

    def flatten(g, f, xx, zz):
        block = jnp.concatenate([g[zz, xx, 0].astype(F32), g[zz, xx, 1].astype(F32)], axis=0)
        f[xx, pl.ds(pl.multiple_of(48 * zz, 48), 48), :] = block.astype(BF16)

    def flatten_own(g, i, f, k):
        zz = zs(way * k)
        if k > 0:
            slot = g.at[zz, xl] if k < FAR else g.at[zz, xl, 1 - core]
            recv(slot, sib_send.at[i, k], sib_recv.at[i, k], sibling)
        flatten(g, f, xl, zz)
        if 0 < k < FAR:
            flatten(g, f, xl, zs(-way * k))

    def flatten_partner(g, i, f, k):
        zz = zs(way * k)
        slot = g.at[zz, 1 - xl] if 0 < k < FAR else g.at[zz, 1 - xl, 1 - core]
        recv(slot, sib_send.at[i, FAR + 1 + k], sib_recv.at[i, FAR + 1 + k], sibling)
        flatten(g, f, 1 - xl, zz)
        if 0 < k < FAR:
            flatten(g, f, 1 - xl, zs(-way * k))

    def small_sum(buf, j, a, b):
        lane = lax.broadcasted_iota(jnp.int32, (24, 128), 1)
        buf[n] = jnp.where(lane == 0, a, jnp.where(lane == 1, b, 0.0))
        for k, p in enumerate(n_peers):
            send(buf.at[n], buf.at[n], st_send.at[j, k], st_recv.at[j, k], p)

    def small_total(buf, j):
        for k in range(NARROW - 1):
            frm = (n - 1 - k + NARROW) % NARROW
            recv(buf.at[frm], st_send.at[j, k], st_recv.at[j, k], (w, frm))
        total = jnp.sum(buf[...], axis=0)
        return total[:, 0:1] / full_width, total[:, 1:2] / full_width

    gather_own(cg, 0)
    x = x_ref[...].astype(F32)
    small_sum(st, 0, jnp.sum(x, axis=1, keepdims=True), jnp.sum(x * x, axis=1, keepdims=True))
    gather_out(cg, 0)
    row_mean, row_sq = small_total(st, 0)
    row_rstd = lax.rsqrt(row_sq - row_mean * row_mean + EPS)
    ng[z, xl, core] = ((x_ref[...].astype(F32) - row_mean) * row_rstd * ngain).astype(BF16)
    gather_own(ng, 1)

    every = slice(None)
    even = ((0, 1, 2), (1, 2, 0), (2, 0, 1))
    rs_orders = (even,) * 6
    ag_orders = (even,) * 4

    def at(ref, half, part, fixed):
        return ref.at[(half,) + tuple(fixed.get(d, every) for d in range(3)) + (part,)]

    def rs_first(p, half, b, rnd):
        s1, r1 = b[0], b[1]
        for r in range(3):
            d = rs_orders[rnd][r][0]
            s1[r] = at(p, half, r, {d: 1 - bits[d]})[...].astype(BF16)
            send(s1.at[r], r1.at[r], rs_send.at[rnd, 0, r], rs_recv.at[rnd, 0, r], cube[d])

    def rs_second(p, half, b, rnd):
        r1, a1, s2, r2 = b[1:5]
        for r in range(3):
            d, e, _ = rs_orders[rnd][r]
            recv(r1.at[r], rs_send.at[rnd, 0, r], rs_recv.at[rnd, 0, r], cube[d])
            rest = [i for i in range(3) if i != d]
            pick = lambda v: (r,) + tuple(v if i == e else every for i in rest)
            away, stay = 1 - bits[e], bits[e]
            s2[r] = (
                at(p, half, r, {d: bits[d], e: away})[...] + r1.at[pick(away)][...].astype(F32)
            ).astype(BF16)
            send(s2.at[r], r2.at[r], rs_send.at[rnd, 1, r], rs_recv.at[rnd, 1, r], cube[e])
            a1[r] = at(p, half, r, {d: bits[d], e: stay})[...] + r1.at[pick(stay)][...].astype(F32)

    def rs_third(half, b, rnd):
        a1, r2, a2, s3, r3 = b[2], b[4], b[5], b[6], b[7]
        for r in range(3):
            _, e, f = rs_orders[rnd][r]
            recv(r2.at[r], rs_send.at[rnd, 1, r], rs_recv.at[rnd, 1, r], cube[e])
            away, stay = (r, 1 - bits[f]), (r, bits[f])
            s3[r] = (a1[away] + r2[away].astype(F32)).astype(BF16)
            send(s3.at[r], r3.at[r], rs_send.at[rnd, 2, r], rs_recv.at[rnd, 2, r], cube[f])
            a2[r] = a1[stay] + r2[stay].astype(F32)

    def rs_last(b, rnd):
        a2, r3 = b[5], b[7]
        for r in range(3):
            f = rs_orders[rnd][r][2]
            recv(r3.at[r], rs_send.at[rnd, 2, r], rs_recv.at[rnd, 2, r], cube[f])
            a2[r] = a2[r] + r3[r].astype(F32)

    def cot_products(half):
        lhs = lambda: cf[half]
        shape = lambda c: (2, 2, 2, 3, 16, c)
        pd[half, :, :, :, :, :, 0:128] = nt(lhs(), wdn[0:128, :]).reshape(shape(128))
        for j in range(3):
            lo = 128 + 256 * j
            pd[half, :, :, :, :, :, lo:lo + 256] = nt(lhs(), wdn[lo:lo + 256, :]).reshape(shape(256))

    def query_products(half):
        shape = lambda c: (2, 2, 2, 3, 16, c)
        pq[half, :, :, :, :, :, 0:256] = nn(nf[half], wf[:, 0:256]).reshape(shape(256))
        pq[half, :, :, :, :, :, 256:384] = nn(nf[half], wf[:, 256:384]).reshape(shape(128))

    def up_products(half):
        for j in range(3):
            lo = 256 * j
            pu[half, :, :, :, :, :, lo:lo + 256] = nn(nf[half], wf[:, 384 + lo:640 + lo]).reshape((2, 2, 2, 3, 16, 256))

    def ag(buf, half, rnd, step):
        for r in range(3):
            order = ag_orders[rnd][r][::-1]
            src = at(buf, half, r, {d: bits[d] for d in order[step:]})
            send(src, src, ag_send.at[rnd, step, r], ag_recv.at[rnd, step, r], cube[order[step]])

    def ag_wait(buf, half, rnd, step):
        for r in range(3):
            order = ag_orders[rnd][r][::-1]
            fixed = {d: bits[d] for d in order[step:]}
            fixed[order[step]] = 1 - bits[order[step]]
            recv(
                at(buf, half, r, fixed), ag_send.at[rnd, step, r], ag_recv.at[rnd, step, r], cube[order[step]]
            )

    mine = (bits[0], bits[1], bits[2])
    theirs = 1 - xl

    def gelu(half, b_up, b_d):
        up = b_up[5][...]
        sq = up * up
        t = jnp.tanh(GELU_C * up * (1.0 + GELU_A * sq))
        gh[(half,) + mine] = (0.5 * up * (1.0 + t)).astype(BF16)
        slope = 0.5 * (1.0 + t) + 0.5 * up * (1.0 - t * t) * (GELU_C * (1.0 + 3.0 * GELU_A * sq))
        gp[(half,) + mine] = (b_d[5][:, :, 128:896] * slope).astype(BF16)

    gather_out(ng, 1)
    gather_line(cg, 0, 1)
    gather_line(cg, 0, 2)
    gather_line(cg, 0, 3)
    gather_line(cg, 0, 4)
    gather_x(cg, 0, 0)
    gather_x(cg, 0, 1)
    flatten_own(cg, 0, cf, 0)
    flatten_own(cg, 0, cf, 1)
    flatten_own(cg, 0, cf, 2)
    gather_x(cg, 0, 2)
    flatten_own(cg, 0, cf, 3)
    flatten_own(cg, 0, cf, 4)
    wcopies[0].wait()
    wcopies[1].wait()
    cot_products(xl)
    rs_first(pd, xl, bde, 0)

    gather_line(ng, 1, 1)
    gather_x(cg, 0, 3)
    gather_x(cg, 0, 4)
    gather_line(ng, 1, 2)
    gather_x(ng, 1, 0)
    gather_line(ng, 1, 3)
    gather_line(ng, 1, 4)
    gather_x(ng, 1, 1)
    for k in range(FAR + 1):
        flatten_partner(cg, 0, cf, k)
    gather_x(ng, 1, 2)
    cot_products(theirs)
    rs_first(pd, theirs, bdl, 1)

    gather_x(ng, 1, 3)
    gather_x(ng, 1, 4)
    for k in range(FAR + 1):
        flatten_own(ng, 1, nf, k)
    for c in wcopies[2:]:
        c.wait()
    query_products(xl)
    rs_first(pq, xl, bqe, 2)
    rs_second(pd, xl, bde, 0)
    up_products(xl)
    rs_first(pu, xl, bue, 3)
    for k in range(FAR + 1):
        flatten_partner(ng, 1, nf, k)
    query_products(theirs)
    rs_first(pq, theirs, bql, 4)
    rs_second(pd, theirs, bdl, 1)
    up_products(theirs)
    rs_first(pu, theirs, bul, 5)

    rs_second(pq, xl, bqe, 2)
    rs_third(xl, bde, 0)
    rs_second(pq, theirs, bql, 4)
    rs_second(pu, xl, bue, 3)
    rs_third(theirs, bdl, 1)
    rs_third(xl, bqe, 2)
    rs_second(pu, theirs, bul, 5)
    rs_third(theirs, bql, 4)
    rs_third(xl, bue, 3)
    rs_last(bde, 0)
    rs_last(bdl, 1)
    rs_last(bqe, 2)
    rs_third(theirs, bul, 5)
    rs_last(bql, 4)
    for half, b_q, b_d in ((xl, bqe, bde), (theirs, bql, bdl)):
        ga[(half,) + mine + (every, every, pl.ds(0, 384))] = b_q[5][...].astype(BF16)
        ga[(half,) + mine + (every, every, pl.ds(384, 128))] = b_d[5][:, :, 0:128].astype(BF16)
    ag(ga, every, 0, 0)
    rs_last(bue, 3)
    gelu(xl, bue, bde)
    rs_last(bul, 5)
    gelu(theirs, bul, bdl)
    ag(gp, theirs, 1, 0)
    ag(gp, xl, 2, 0)
    for step in range(2):
        for buf, half, rnd in ((ga, every, 0), (gp, theirs, 1), (gp, xl, 2)):
            ag_wait(buf, half, rnd, step)
            ag(buf, half, rnd, step + 1)
    ag(gh, every, 3, 0)
    ag_wait(ga, every, 0, 2)

    scale = HEAD ** (-0.5)
    qgain = qgain_ref[...]
    kgain = kgain_ref[...]
    gain_sums = [jnp.zeros((1, HEAD), F32), jnp.zeros((1, HEAD), F32)]

    def attention(image):
        places = [(b % 6 // 3, b // 6, b % 3) for b in range(image * 16, image * 16 + 16)]
        load = lambda lo: jnp.concatenate(
            [ga[xx, c // 4, c // 2 % 2, c % 2, r, :, lo:lo + 128] for xx, c, r in places], axis=0
        )

        def store(ref, lo, value):
            for i, (xx, c, r) in enumerate(places):
                ref[xx, c, r, :, lo:lo + 128] = value[16 * i:16 * i + 16]

        q_unit, q_rstd = head_norm(load(0).astype(F32))
        k_unit, k_rstd = head_norm(load(128).astype(F32))
        values = load(256)
        d_att = load(384)
        q_normed = (q_unit * qgain).astype(BF16)
        k_normed = (k_unit * kgain).astype(BF16)
        exponent = jnp.exp(nt(q_normed, k_normed) * scale)
        probs = exponent / jnp.sum(exponent, axis=-1, keepdims=True)
        low = probs.astype(BF16)
        store(att, 0, nn(low, values).astype(BF16))
        d_probs = nt(d_att, values)
        store(dqkv, 256, tn(low, d_att).astype(BF16))
        d_scores = (probs * (d_probs - jnp.sum(probs * d_probs, axis=-1, keepdims=True))).astype(BF16)
        d_qnorm = nn(d_scores, k_normed) * scale
        d_knorm = tn(d_scores, q_normed) * scale
        gain_sums[0] = gain_sums[0] + jnp.sum(d_qnorm * q_unit, axis=0, keepdims=True)
        gain_sums[1] = gain_sums[1] + jnp.sum(d_knorm * k_unit, axis=0, keepdims=True)
        store(dqkv, 0, norm_back(d_qnorm * qgain, q_unit, q_rstd).astype(BF16))
        store(dqkv, 128, norm_back(d_knorm * kgain, k_unit, k_rstd).astype(BF16))

    for image in range(3):
        attention(image)

    gain_rows = []
    ones = jnp.ones((8, 256), BF16)
    tile_row = lax.broadcasted_iota(jnp.int32, (8, 384), 0)
    tile_parts = []

    def products(half, e):
        sum_gain = sum_normed = jnp.zeros((8, 384), F32)
        d_heads = lambda: dqkv[half].reshape(384, 384)
        d_up = lambda: gp[half].reshape(384, 768)
        for j in range(3):
            cols = slice(256 * j, 256 * j + 256)
            res = nt(d_heads(), wf[cols, 0:384]) + nt(d_up(), wf[cols, 384:1152])
            dp[e, :, :, :, cols] = res.reshape(Z, 2, 24, 256)
            with_normed = res * nf[half, :, cols].astype(F32)
            gain_rows.append(jnp.sum(with_normed, axis=0, keepdims=True) / ngain[:, cols])
            sum_gain = sum_gain + nt(ones, (res * ngain[:, cols]).astype(BF16))
            sum_normed = sum_normed + nt(ones, with_normed.astype(BF16))
        tile_parts.append(
            jnp.where(tile_row == 2 * half, sum_gain, jnp.where(tile_row == 2 * half + 1, sum_normed, 0.0))
        )
        sib_s[e, FAR - 1, 0] = dp[e, zs(FAR), 1 - core].astype(BF16)
        sib_s[e, FAR - 1, 1] = dp[e, z, 1 - core].astype(BF16)
        for k in range(FAR, 0, -1):
            if k < FAR:
                sib_s[e, k - 1] = dp[e, zs(-way * k)].astype(BF16)
            send(sib_s.at[e, k - 1], sib_r.at[e, k - 1], c_send.at[e, k - 1], c_recv.at[e, k - 1], sibling)

    def from_sibling(e, k):
        recv(sib_r.at[e, k - 1], c_send.at[e, k - 1], c_recv.at[e, k - 1], sibling)

    def pair(e, k):
        return dp[e, zs(way * k)] + sib_r[e, k - 1].astype(F32)

    def far(e):
        return dp[e, zs(FAR), core] + sib_r[e, FAR - 1, 0].astype(F32)

    def near(e):
        return dp[e, z, core] + sib_r[e, FAR - 1, 1].astype(F32)

    ag_wait(gp, theirs, 1, 2)
    ag_wait(gh, every, 3, 0)
    ag(gh, every, 3, 1)
    products(theirs, 0)
    for k in range(FAR, 0, -1):
        from_sibling(0, k)
        if k == FAR:
            x_s[FAR - 1, 0] = far(0).astype(BF16)
            x_s[FAR - 1, 1] = near(0).astype(BF16)
        else:
            x_s[k - 1] = pair(0, k).astype(BF16)
        send(x_s.at[k - 1], x_r.at[k - 1], x_send.at[k - 1], x_recv.at[k - 1], xpartner)

    ag_wait(gp, xl, 2, 2)
    ag_wait(gh, every, 3, 1)
    ag(gh, every, 3, 2)
    products(xl, 1)
    gain_rows = [
        (gain_rows[j] + gain_rows[j + 3])[:, 128 * i:128 * i + 128] for j in range(3) for i in range(2)
    ]
    gain_tile = jnp.concatenate(gain_rows + gain_sums, axis=0)
    gain_tile = jnp.concatenate([gain_tile[0:4], gain_tile[4:8], jnp.zeros((4, 128), F32)], axis=1)
    tile[0] = tile_parts[0] + tile_parts[1] + jnp.concatenate([jnp.zeros((4, 384), F32), gain_tile], axis=0)
    for k in range(1, Z):
        send(tile.at[0], gz.at[k - 1], gz_send.at[k - 1], gz_recv.at[k - 1], z_peers[k - 1])
    for k in range(FAR, 0, -1):
        recv(x_r.at[k - 1], x_send.at[k - 1], x_recv.at[k - 1], xpartner)
        from_sibling(1, k)
        if k == FAR:
            z_s[FAR - 1, 0] = (far(1) + x_r[FAR - 1, 0].astype(F32)).astype(BF16)
            src, dst = z_s.at[FAR - 1, 0], z_r.at[FAR - 1, 0]
        else:
            z_s[k - 1] = (pair(1, k) + x_r[k - 1].astype(F32)).astype(BF16)
            src, dst = z_s.at[k - 1], z_r.at[k - 1]
        send(src, dst, z_send.at[k], z_recv.at[k], (dev(zs(way * k), xl, core), n))
    fin[core] = near(1) + x_r[FAR - 1, 1].astype(F32)
    for j in range(3):
        cols = slice(256 * j, 256 * j + 256)
        left = nf[:, :, cols].reshape(768, 256)
        gu[cols, :] = tn(left, gp[...].reshape(768, 768)).astype(BF16)
        res = tn(left, dqkv[...].reshape(768, 384)).astype(BF16)
        gq[cols, :] = res[:, 0:128]
        gk[cols, :] = res[:, 128:256]
        gv[cols, :] = res[:, 256:384]
    for k in range(1, Z):
        recv(gz.at[k - 1], gz_send.at[k - 1], gz_recv.at[k - 1], z_peers[Z - 1 - k])
    tile[1] = tile[0] + jnp.sum(gz[...], axis=0)
    for j in range(3):
        send(tile.at[1], gquad.at[j], gq_send.at[j], gq_recv.at[j], quad[j])
    ag_wait(gh, every, 3, 2)
    for j in range(3):
        cols = slice(256 * j, 256 * j + 256)
        hidden = gh[:, :, :, :, :, :, cols].reshape(768, 256)
        gd[cols, :] = tn(hidden, cf[...].reshape(768, 768)).astype(BF16)
    for j in range(3):
        recv(gquad.at[j], gq_send.at[j], gq_recv.at[j], quad[j])
    wide_total = tile[1] + gquad[0] + gquad[1] + gquad[2]
    rows[0] = wide_total
    gains[0:4] = wide_total[4:8, 0:128]
    gains[4:8] = wide_total[4:8, 128:256]
    for k, p in enumerate(n_peers):
        send(rows.at[0], rows.at[k + 1], st_send.at[1, k], st_recv.at[1, k], p)
    go[...] = tn(att[...].reshape(768, 128), cf[...].reshape(768, 768)).astype(BF16)

    recv(z_r.at[FAR - 1, 0], z_send.at[FAR], z_recv.at[FAR], (dev(zs(FAR), xl, core), n))
    for k in range(1, FAR):
        recv(z_r.at[k - 1], z_send.at[k], z_recv.at[k], (dev(zs(-way * k), xl, core), n))
    fin[1 - core] = sum(z_r[k, 1 - core].astype(F32) for k in range(FAR - 1))
    fin_s[...] = fin[1 - core].astype(BF16)
    send(fin_s, fin_r, f_sem.at[0], f_sem.at[1], sibling)

    d_own = fin[core] + z_r[FAR - 1, 0].astype(F32) + sum(z_r[k, core].astype(F32) for k in range(FAR - 1))
    recv(fin_r, f_sem.at[0], f_sem.at[1], sibling)
    d_normed = d_own + fin_r[...].astype(F32)
    d_unit = d_normed * ngain
    unit = (x_ref[...].astype(F32) - row_mean) * row_rstd

    for k in range(NARROW - 1):
        recv(rows.at[k + 1], st_send.at[1, k], st_recv.at[1, k], (w, (n - 1 - k + NARROW) % NARROW))
    tile[2] = jnp.sum(rows[...], axis=0)
    own_row = lax.broadcasted_iota(jnp.int32, (24, 384), 0) + (48 * z + 24 * core)
    own_row = own_row == lax.broadcasted_iota(jnp.int32, (24, 384), 1)
    pick_row = lambda i: jnp.sum(jnp.where(own_row, tile[2, pl.ds(2 * xl + i, 1), :], 0.0), axis=1, keepdims=True) / full_width
    first, second = pick_row(0), pick_row(1)
    dx[...] = (cot_ref[...].astype(F32) + row_rstd * (d_unit - first - unit * second)).astype(BF16)

    for c in pending:
        c.wait_send()


def hand_over(*refs):
    srcs, gains_ref, outs, (ngain_ref, qg_ref, kg_ref), sem = refs[:7], refs[7], refs[8:15], refs[15:18], refs[18]
    copies = [pltpu.make_async_copy(s, o, sem.at[i]) for i, (s, o) in enumerate(zip(srcs, outs))]
    for c in copies:
        c.start()
    for i in range(6):
        ngain_ref[pl.ds(128 * i, 128)] = gains_ref[i, :]
    qg_ref[...] = gains_ref[6, :]
    kg_ref[...] = gains_ref[7, :]
    for c in copies:
        c.wait()


def per_device(inputs, cotangent, norm_gain, q_gain, k_gain, w_query, w_key, w_value, w_out, w_up, w_down):
    full_width = inputs.shape[1] * NARROW
    vm = pl.BlockSpec(memory_space=pltpu.VMEM)
    anywhere = pl.BlockSpec(memory_space=pl.ANY)
    v = pltpu.VMEM
    dma = pltpu.SemaphoreType.DMA

    def rs_buffers(c):
        return [
            v((3, 2, 2, 16, c), BF16), v((3, 2, 2, 16, c), BF16), v((3, 2, 16, c), F32),
            v((3, 2, 16, c), BF16), v((3, 2, 16, c), BF16), v((3, 16, c), F32),
            v((3, 16, c), BF16), v((3, 16, c), BF16),
        ]

    grads = [(24, 768), (768, 128), (768, 128), (768, 128), (128, 768), (768, 768), (768, 768)]
    cube = (2, 2, 2, 2, 3, 16)
    scratch = [
        v((768, 1152), BF16), v((896, 768), BF16),
        v((Z, 2, 2, 24, 768), BF16), v((Z, 2, 2, 24, 768), BF16), v((2, 384, 768), BF16), v((2, 384, 768), BF16),
        v((*cube, 896), F32), v((*cube, 384), F32), v((*cube, 768), F32),
        rs_buffers(896), rs_buffers(896), rs_buffers(384), rs_buffers(384), rs_buffers(768), rs_buffers(768),
        v((*cube, 512), BF16), v((*cube, 768), BF16), v((*cube, 768), BF16),
        v((2, 8, 3, 16, 384), BF16), v((2, 8, 3, 16, 128), BF16),
        v((2, Z, 2, 24, 768), F32), v((2, 4, 2, 24, 768), BF16), v((2, 4, 2, 24, 768), BF16),
        v((4, 2, 24, 768), BF16), v((4, 2, 24, 768), BF16), v((4, 2, 24, 768), BF16), v((4, 2, 24, 768), BF16),
        v((2, 24, 768), F32), v((24, 768), BF16), v((24, 768), BF16),
        v((NARROW, 24, 128), F32), v((NARROW, 8, 384), F32),
        v((3, 8, 384), F32), v((3, 8, 384), F32), v((Z - 1, 8, 384), F32),
        dma((6,)), dma((2, 10)), dma((2, 10)), dma((2, 5)), dma((2, 5)), dma((2, 5)), dma((2, 5)),
        dma((6, 3, 3)), dma((6, 3, 3)), dma((4, 3, 3)), dma((4, 3, 3)),
        dma((2, NARROW - 1)), dma((2, NARROW - 1)),
        dma((2, 4)), dma((2, 4)), dma((4,)), dma((4,)), dma((5,)), dma((5,)), dma((2,)), dma((3,)), dma((3,)),
        dma((Z - 1,)), dma((Z - 1,)),
    ]
    grad_shapes = [jax.ShapeDtypeStruct(g, BF16) for g in grads]
    outs = pl.pallas_call(
        functools.partial(kernel, full_width),
        out_shape=(*[v(g, BF16) for g in grads], v((8, 128), F32)),
        in_specs=[vm] * 5 + [pl.BlockSpec(memory_space=pltpu.HBM)] * 6,
        out_specs=[vm] * 8,
        scratch_shapes=scratch,
        compiler_params=pltpu.CompilerParams(
            collective_id=0, has_side_effects=True, vmem_limit_bytes=56 * 1024 * 1024
        ),
        name="layer",
    )(
        inputs, cotangent, norm_gain, q_gain.reshape(1, -1), k_gain.reshape(1, -1),
        w_query, w_key, w_value, w_out, w_up, w_down,
    )
    return pl.pallas_call(
        hand_over,
        out_shape=(
            *grad_shapes,
            jax.ShapeDtypeStruct((768,), F32), jax.ShapeDtypeStruct((128,), F32), jax.ShapeDtypeStruct((128,), F32),
        ),
        in_specs=[vm] * 8,
        out_specs=[anywhere] * 7 + [vm] * 3,
        scratch_shapes=[dma((7,))],
        name="hand_over",
    )(*[pltpu.with_memory_space_constraint(o, pltpu.VMEM) for o in outs])


def solution(mesh):
    return jax.shard_map(
        per_device,
        mesh=mesh,
        in_specs=(
            P("wide", "narrow"), P("wide", "narrow"), P("narrow"), P(), P(),
            P("narrow", "wide"), P("narrow", "wide"), P("narrow", "wide"), P("wide", "narrow"),
            P("narrow", "wide"), P("wide", "narrow"),
        ),
        out_specs=(
            P("wide", "narrow"),
            P("narrow", "wide"), P("narrow", "wide"), P("narrow", "wide"), P("wide", "narrow"),
            P("narrow", "wide"), P("wide", "narrow"),
            P("narrow"), P(), P(),
        ),
        check_vma=False,
    )
```

```python
import functools
import math

import jax
import jax.numpy as jnp
from jax import lax
from jax.experimental import pallas as pl
from jax.experimental.pallas import tpu as pltpu
from jax.sharding import PartitionSpec as P

MESH = pl.DeviceIdType.MESH
F32 = jnp.float32
BF16 = jnp.bfloat16
EPS = 1e-06
PATCHES = 256
HEAD = 128
Z = 8
FAR = Z // 2
WIDE = 32
NARROW = 8
GELU_C = math.sqrt(2.0 / math.pi)
GELU_A = 0.044715


def nn(a, b):
    return lax.dot_general(a, b, (((1,), (0,)), ((), ())), preferred_element_type=F32)


def nt(a, b):
    return lax.dot_general(a, b, (((1,), (1,)), ((), ())), preferred_element_type=F32)


def tn(a, b):
    return lax.dot_general(a, b, (((0,), (0,)), ((), ())), preferred_element_type=F32)


def head_norm(matrix):
    centre = jnp.mean(matrix, axis=-1, keepdims=True)
    shifted = matrix - centre
    inv_std = lax.rsqrt(jnp.mean(shifted * shifted, axis=-1, keepdims=True) + EPS)
    return shifted * inv_std, inv_std


def norm_back(upstream, normal, inv_std):
    first = jnp.mean(upstream, axis=-1, keepdims=True)
    second = jnp.mean(upstream * normal, axis=-1, keepdims=True)
    return inv_std * (upstream - first - normal * second)


def kernel(
    full_width,
    x_ref, cot_ref, ngain_ref, qgain_ref, kgain_ref,
    wq_hbm, wk_hbm, wv_hbm, wo_hbm, wu_hbm, wd_hbm,
    dx, gq, gk, gv, go, gu, gd, gains,
    wf, wdn,
    cg, ng, cf, nf,
    pd, pq, pu,
    bde, bdl, bqe, bql, bul, bue,
    ga, gp, gh, dqkv, att,
    dp, sib_s, sib_r, x_s, x_r, z_s, z_r, fin, fin_s, fin_r,
    st, rows, tile, gquad, gz,
    wsem, sib_send, sib_recv, xp_send, xp_recv, line_send, line_recv,
    rs_send, rs_recv, ag_send, ag_recv, st_send, st_recv,
    c_send, c_recv, x_send, x_recv, z_send, z_recv, f_sem, gq_send, gq_recv, gz_send, gz_recv,
):
    w = lax.axis_index("wide")
    n = lax.axis_index("narrow")
    z = w // 4
    xl = (w // 2) % 2
    core = w % 2
    xh = n // 4
    y = n % 4
    way = 1 - 2 * core
    zs = lambda k: (z + k + Z) % Z
    dev = lambda zz, xx, cc: zz * 4 + xx * 2 + cc

    bits = (((y + 1) // 2) % 2, y // 2, xh)
    cube = (
        (w, xh * 4 + y + 1 - 2 * (y % 2)),
        (w, xh * 4 + 3 - y),
        (w, (1 - xh) * 4 + y),
    )
    sibling = (dev(z, xl, 1 - core), n)
    quad = (sibling, (dev(z, 1 - xl, core), n), (dev(z, 1 - xl, 1 - core), n))
    quad_at = ((xl, 1 - core), (1 - xl, core), (1 - xl, 1 - core))
    xpartner = quad[1]
    z_peers = [(dev(zs(k), xl, core), n) for k in range(1, Z)]
    n_peers = [(w, (n + k) % NARROW) for k in range(1, NARROW)]

    pending = []

    def send(src, dst, ssem, rsem, to):
        copy = pltpu.make_async_remote_copy(
            src_ref=src, dst_ref=dst, send_sem=ssem, recv_sem=rsem, device_id=to, device_id_type=MESH
        )
        copy.start()
        pending.append(copy)

    def recv(ref, ssem, rsem, frm):
        pltpu.make_async_remote_copy(
            src_ref=ref, dst_ref=ref, send_sem=ssem, recv_sem=rsem, device_id=frm, device_id_type=MESH
        ).wait_recv()

    wcopies = []
    for i, (src, dst) in enumerate((
        (wo_hbm, wdn.at[pl.ds(0, 128)]),
        (wd_hbm, wdn.at[pl.ds(128, 768)]),
        (wq_hbm, wf.at[:, pl.ds(0, 128)]),
        (wk_hbm, wf.at[:, pl.ds(128, 128)]),
        (wv_hbm, wf.at[:, pl.ds(256, 128)]),
        (wu_hbm, wf.at[:, pl.ds(384, 768)]),
    )):
        c = pltpu.make_async_copy(src, dst, wsem.at[i])
        c.start()
        wcopies.append(c)

    peers = [*quad, *z_peers, *n_peers]
    barrier = pltpu.get_barrier_semaphore()
    for p in peers:
        pl.semaphore_signal(barrier, inc=1, device_id=p, device_id_type=MESH)
    ngain = jnp.concatenate([ngain_ref[pl.ds(128 * i, 128)].reshape(1, 128) for i in range(6)], axis=1)
    cg[z, xl, core] = cot_ref[...]
    pl.semaphore_wait(barrier, len(peers))

    def gather_own(g, i):
        slot = g.at[z, xl, core]
        send(slot, slot, sib_send.at[i, 0], sib_recv.at[i, 0], sibling)
        send(slot, slot, xp_send.at[i, 0], xp_recv.at[i, 0], xpartner)

    def gather_out(g, i):
        recv(g.at[z, xl, 1 - core], sib_send.at[i, 0], sib_recv.at[i, 0], sibling)
        for k in range(1, FAR + 1):
            slot = g.at[z, xl] if k < FAR else g.at[z, xl, core]
            send(slot, slot, line_send.at[i, k], line_recv.at[i, k], (dev(zs(way * k), xl, core), n))

    def gather_line(g, i, k):
        zz = zs(-way * k)
        slot = g.at[zz, xl] if k < FAR else g.at[zz, xl, core]
        recv(slot, line_send.at[i, k], line_recv.at[i, k], (dev(zz, xl, core), n))
        send(slot, slot, sib_send.at[i, k], sib_recv.at[i, k], sibling)
        send(slot, slot, xp_send.at[i, k], xp_recv.at[i, k], xpartner)

    def gather_x(g, i, k):
        zz = zs(-way * k)
        slot = g.at[zz, 1 - xl] if 0 < k < FAR else g.at[zz, 1 - xl, core]
        recv(slot, xp_send.at[i, k], xp_recv.at[i, k], xpartner)
        send(slot, slot, sib_send.at[i, FAR + 1 + k], sib_recv.at[i, FAR + 1 + k], sibling)

    def flatten(g, f, xx, zz):
        block = jnp.concatenate([g[zz, xx, 0].astype(F32), g[zz, xx, 1].astype(F32)], axis=0)
        f[xx, pl.ds(pl.multiple_of(48 * zz, 48), 48), :] = block.astype(BF16)

    def flatten_own(g, i, f, k):
        zz = zs(way * k)
        if k > 0:
            slot = g.at[zz, xl] if k < FAR else g.at[zz, xl, 1 - core]
            recv(slot, sib_send.at[i, k], sib_recv.at[i, k], sibling)
        flatten(g, f, xl, zz)
        if 0 < k < FAR:
            flatten(g, f, xl, zs(-way * k))

    def flatten_partner(g, i, f, k):
        zz = zs(way * k)
        slot = g.at[zz, 1 - xl] if 0 < k < FAR else g.at[zz, 1 - xl, 1 - core]
        recv(slot, sib_send.at[i, FAR + 1 + k], sib_recv.at[i, FAR + 1 + k], sibling)
        flatten(g, f, 1 - xl, zz)
        if 0 < k < FAR:
            flatten(g, f, 1 - xl, zs(-way * k))

    def small_sum(buf, j, a, b):
        lane = lax.broadcasted_iota(jnp.int32, (24, 128), 1)
        buf[n] = jnp.where(lane == 0, a, jnp.where(lane == 1, b, 0.0))
        for k, p in enumerate(n_peers):
            send(buf.at[n], buf.at[n], st_send.at[j, k], st_recv.at[j, k], p)

    def small_total(buf, j):
        for k in range(NARROW - 1):
            frm = (n - 1 - k + NARROW) % NARROW
            recv(buf.at[frm], st_send.at[j, k], st_recv.at[j, k], (w, frm))
        total = jnp.sum(buf[...], axis=0)
        return total[:, 0:1] / full_width, total[:, 1:2] / full_width

    gather_own(cg, 0)
    x = x_ref[...].astype(F32)
    small_sum(st, 0, jnp.sum(x, axis=1, keepdims=True), jnp.sum(x * x, axis=1, keepdims=True))
    gather_out(cg, 0)
    row_mean, row_sq = small_total(st, 0)
    row_rstd = lax.rsqrt(row_sq - row_mean * row_mean + EPS)
    ng[z, xl, core] = ((x_ref[...].astype(F32) - row_mean) * row_rstd * ngain).astype(BF16)
    gather_own(ng, 1)

    every = slice(None)
    even = ((0, 1, 2), (1, 2, 0), (2, 0, 1))
    rs_orders = (even,) * 6
    ag_orders = (even,) * 4

    def at(ref, half, part, fixed):
        return ref.at[(half,) + tuple(fixed.get(d, every) for d in range(3)) + (part,)]

    def rs_first(p, half, b, rnd):
        s1, r1 = b[0], b[1]
        for r in range(3):
            d = rs_orders[rnd][r][0]
            s1[r] = at(p, half, r, {d: 1 - bits[d]})[...].astype(BF16)
            send(s1.at[r], r1.at[r], rs_send.at[rnd, 0, r], rs_recv.at[rnd, 0, r], cube[d])

    def rs_second(p, half, b, rnd):
        r1, a1, s2, r2 = b[1:5]
        for r in range(3):
            d, e, _ = rs_orders[rnd][r]
            recv(r1.at[r], rs_send.at[rnd, 0, r], rs_recv.at[rnd, 0, r], cube[d])
            rest = [i for i in range(3) if i != d]
            pick = lambda v: (r,) + tuple(v if i == e else every for i in rest)
            away, stay = 1 - bits[e], bits[e]
            s2[r] = (
                at(p, half, r, {d: bits[d], e: away})[...] + r1.at[pick(away)][...].astype(F32)
            ).astype(BF16)
            send(s2.at[r], r2.at[r], rs_send.at[rnd, 1, r], rs_recv.at[rnd, 1, r], cube[e])
            a1[r] = at(p, half, r, {d: bits[d], e: stay})[...] + r1.at[pick(stay)][...].astype(F32)

    def rs_third(half, b, rnd):
        a1, r2, a2, s3, r3 = b[2], b[4], b[5], b[6], b[7]
        for r in range(3):
            _, e, f = rs_orders[rnd][r]
            recv(r2.at[r], rs_send.at[rnd, 1, r], rs_recv.at[rnd, 1, r], cube[e])
            away, stay = (r, 1 - bits[f]), (r, bits[f])
            s3[r] = (a1[away] + r2[away].astype(F32)).astype(BF16)
            send(s3.at[r], r3.at[r], rs_send.at[rnd, 2, r], rs_recv.at[rnd, 2, r], cube[f])
            a2[r] = a1[stay] + r2[stay].astype(F32)

    def rs_last(b, rnd):
        a2, r3 = b[5], b[7]
        for r in range(3):
            f = rs_orders[rnd][r][2]
            recv(r3.at[r], rs_send.at[rnd, 2, r], rs_recv.at[rnd, 2, r], cube[f])
            a2[r] = a2[r] + r3[r].astype(F32)

    def cot_products(half):
        lhs = lambda: cf[half]
        shape = lambda c: (2, 2, 2, 3, 16, c)
        pd[half, :, :, :, :, :, 0:128] = nt(lhs(), wdn[0:128, :]).reshape(shape(128))
        for j in range(3):
            lo = 128 + 256 * j
            pd[half, :, :, :, :, :, lo:lo + 256] = nt(lhs(), wdn[lo:lo + 256, :]).reshape(shape(256))

    def query_products(half):
        shape = lambda c: (2, 2, 2, 3, 16, c)
        pq[half, :, :, :, :, :, 0:256] = nn(nf[half], wf[:, 0:256]).reshape(shape(256))
        pq[half, :, :, :, :, :, 256:384] = nn(nf[half], wf[:, 256:384]).reshape(shape(128))

    def up_products(half):
        for j in range(3):
            lo = 256 * j
            pu[half, :, :, :, :, :, lo:lo + 256] = nn(nf[half], wf[:, 384 + lo:640 + lo]).reshape((2, 2, 2, 3, 16, 256))

    def ag(buf, half, rnd, step):
        for r in range(3):
            order = ag_orders[rnd][r][::-1]
            src = at(buf, half, r, {d: bits[d] for d in order[step:]})
            send(src, src, ag_send.at[rnd, step, r], ag_recv.at[rnd, step, r], cube[order[step]])

    def ag_wait(buf, half, rnd, step):
        for r in range(3):
            order = ag_orders[rnd][r][::-1]
            fixed = {d: bits[d] for d in order[step:]}
            fixed[order[step]] = 1 - bits[order[step]]
            recv(
                at(buf, half, r, fixed), ag_send.at[rnd, step, r], ag_recv.at[rnd, step, r], cube[order[step]]
            )

    mine = (bits[0], bits[1], bits[2])
    theirs = 1 - xl

    def gelu(half, b_up, b_d):
        up = b_up[5][...]
        sq = up * up
        t = jnp.tanh(GELU_C * up * (1.0 + GELU_A * sq))
        gh[(half,) + mine] = (0.5 * up * (1.0 + t)).astype(BF16)
        slope = 0.5 * (1.0 + t) + 0.5 * up * (1.0 - t * t) * (GELU_C * (1.0 + 3.0 * GELU_A * sq))
        gp[(half,) + mine] = (b_d[5][:, :, 128:896] * slope).astype(BF16)

    gather_out(ng, 1)
    gather_line(cg, 0, 1)
    gather_line(cg, 0, 2)
    gather_line(cg, 0, 3)
    gather_line(cg, 0, 4)
    gather_x(cg, 0, 0)
    gather_x(cg, 0, 1)
    flatten_own(cg, 0, cf, 0)
    flatten_own(cg, 0, cf, 1)
    flatten_own(cg, 0, cf, 2)
    gather_x(cg, 0, 2)
    flatten_own(cg, 0, cf, 3)
    flatten_own(cg, 0, cf, 4)
    wcopies[0].wait()
    wcopies[1].wait()
    cot_products(xl)
    rs_first(pd, xl, bde, 0)

    gather_line(ng, 1, 1)
    gather_x(cg, 0, 3)
    gather_x(cg, 0, 4)
    gather_line(ng, 1, 2)
    gather_x(ng, 1, 0)
    gather_line(ng, 1, 3)
    gather_line(ng, 1, 4)
    gather_x(ng, 1, 1)
    for k in range(FAR + 1):
        flatten_partner(cg, 0, cf, k)
    gather_x(ng, 1, 2)
    cot_products(theirs)
    rs_first(pd, theirs, bdl, 1)

    gather_x(ng, 1, 3)
    gather_x(ng, 1, 4)
    for k in range(FAR + 1):
        flatten_own(ng, 1, nf, k)
    for c in wcopies[2:]:
        c.wait()
    query_products(xl)
    rs_first(pq, xl, bqe, 2)
    rs_second(pd, xl, bde, 0)
    up_products(xl)
    rs_first(pu, xl, bue, 3)
    for k in range(FAR + 1):
        flatten_partner(ng, 1, nf, k)
    query_products(theirs)
    rs_first(pq, theirs, bql, 4)
    rs_second(pd, theirs, bdl, 1)
    up_products(theirs)
    rs_first(pu, theirs, bul, 5)

    rs_second(pq, xl, bqe, 2)
    rs_third(xl, bde, 0)
    rs_second(pq, theirs, bql, 4)
    rs_second(pu, xl, bue, 3)
    rs_third(theirs, bdl, 1)
    rs_third(xl, bqe, 2)
    rs_second(pu, theirs, bul, 5)
    rs_third(theirs, bql, 4)
    rs_third(xl, bue, 3)
    rs_last(bde, 0)
    rs_last(bdl, 1)
    rs_last(bqe, 2)
    rs_third(theirs, bul, 5)
    rs_last(bql, 4)
    for half, b_q, b_d in ((xl, bqe, bde), (theirs, bql, bdl)):
        ga[(half,) + mine + (every, every, pl.ds(0, 384))] = b_q[5][...].astype(BF16)
        ga[(half,) + mine + (every, every, pl.ds(384, 128))] = b_d[5][:, :, 0:128].astype(BF16)
    ag(ga, every, 0, 0)
    rs_last(bue, 3)
    gelu(xl, bue, bde)
    rs_last(bul, 5)
    gelu(theirs, bul, bdl)
    ag(gp, theirs, 1, 0)
    ag(gp, xl, 2, 0)
    ag(gh, every, 3, 0)
    for step in range(2):
        for buf, half, rnd in ((ga, every, 0), (gp, theirs, 1), (gp, xl, 2)):
            ag_wait(buf, half, rnd, step)
            ag(buf, half, rnd, step + 1)
    ag_wait(gh, every, 3, 0)
    ag(gh, every, 3, 1)
    ag_wait(ga, every, 0, 2)

    scale = HEAD ** (-0.5)
    qgain = qgain_ref[...]
    kgain = kgain_ref[...]
    gain_sums = [jnp.zeros((1, HEAD), F32), jnp.zeros((1, HEAD), F32)]

    def attention(image):
        places = [(b % 6 // 3, b // 6, b % 3) for b in range(image * 16, image * 16 + 16)]
        load = lambda lo: jnp.concatenate(
            [ga[xx, c // 4, c // 2 % 2, c % 2, r, :, lo:lo + 128] for xx, c, r in places], axis=0
        )

        def store(ref, lo, value):
            for i, (xx, c, r) in enumerate(places):
                ref[xx, c, r, :, lo:lo + 128] = value[16 * i:16 * i + 16]

        q_unit, q_rstd = head_norm(load(0).astype(F32))
        k_unit, k_rstd = head_norm(load(128).astype(F32))
        values = load(256)
        d_att = load(384)
        q_normed = (q_unit * qgain).astype(BF16)
        k_normed = (k_unit * kgain).astype(BF16)
        exponent = jnp.exp(nt(q_normed, k_normed) * scale)
        probs = exponent / jnp.sum(exponent, axis=-1, keepdims=True)
        low = probs.astype(BF16)
        store(att, 0, nn(low, values).astype(BF16))
        d_probs = nt(d_att, values)
        store(dqkv, 256, tn(low, d_att).astype(BF16))
        d_scores = (probs * (d_probs - jnp.sum(probs * d_probs, axis=-1, keepdims=True))).astype(BF16)
        d_qnorm = nn(d_scores, k_normed) * scale
        d_knorm = tn(d_scores, q_normed) * scale
        gain_sums[0] = gain_sums[0] + jnp.sum(d_qnorm * q_unit, axis=0, keepdims=True)
        gain_sums[1] = gain_sums[1] + jnp.sum(d_knorm * k_unit, axis=0, keepdims=True)
        store(dqkv, 0, norm_back(d_qnorm * qgain, q_unit, q_rstd).astype(BF16))
        store(dqkv, 128, norm_back(d_knorm * kgain, k_unit, k_rstd).astype(BF16))

    for image in range(3):
        attention(image)

    gain_rows = []
    ones = jnp.ones((8, 256), BF16)
    tile_row = lax.broadcasted_iota(jnp.int32, (8, 384), 0)
    tile_parts = []

    def products(half, e):
        sum_gain = sum_normed = jnp.zeros((8, 384), F32)
        d_heads = lambda: dqkv[half].reshape(384, 384)
        d_up = lambda: gp[half].reshape(384, 768)
        for j in range(3):
            cols = slice(256 * j, 256 * j + 256)
            res = nt(d_heads(), wf[cols, 0:384]) + nt(d_up(), wf[cols, 384:1152])
            dp[e, :, :, :, cols] = res.reshape(Z, 2, 24, 256)
            with_normed = res * nf[half, :, cols].astype(F32)
            gain_rows.append(jnp.sum(with_normed, axis=0, keepdims=True) / ngain[:, cols])
            sum_gain = sum_gain + nt(ones, (res * ngain[:, cols]).astype(BF16))
            sum_normed = sum_normed + nt(ones, with_normed.astype(BF16))
        tile_parts.append(
            jnp.where(tile_row == 2 * half, sum_gain, jnp.where(tile_row == 2 * half + 1, sum_normed, 0.0))
        )
        sib_s[e, FAR - 1, 0] = dp[e, zs(FAR), 1 - core].astype(BF16)
        sib_s[e, FAR - 1, 1] = dp[e, z, 1 - core].astype(BF16)
        for k in range(FAR, 0, -1):
            if k < FAR:
                sib_s[e, k - 1] = dp[e, zs(-way * k)].astype(BF16)
            send(sib_s.at[e, k - 1], sib_r.at[e, k - 1], c_send.at[e, k - 1], c_recv.at[e, k - 1], sibling)

    def from_sibling(e, k):
        recv(sib_r.at[e, k - 1], c_send.at[e, k - 1], c_recv.at[e, k - 1], sibling)

    def pair(e, k):
        return dp[e, zs(way * k)] + sib_r[e, k - 1].astype(F32)

    def far(e):
        return dp[e, zs(FAR), core] + sib_r[e, FAR - 1, 0].astype(F32)

    def near(e):
        return dp[e, z, core] + sib_r[e, FAR - 1, 1].astype(F32)

    ag_wait(gp, theirs, 1, 2)
    products(theirs, 0)
    for k in range(FAR, 0, -1):
        from_sibling(0, k)
        if k == FAR:
            x_s[FAR - 1, 0] = far(0).astype(BF16)
            x_s[FAR - 1, 1] = near(0).astype(BF16)
        else:
            x_s[k - 1] = pair(0, k).astype(BF16)
        send(x_s.at[k - 1], x_r.at[k - 1], x_send.at[k - 1], x_recv.at[k - 1], xpartner)

    ag_wait(gh, every, 3, 1)
    ag(gh, every, 3, 2)
    ag_wait(gp, xl, 2, 2)
    products(xl, 1)
    gain_rows = [
        (gain_rows[j] + gain_rows[j + 3])[:, 128 * i:128 * i + 128] for j in range(3) for i in range(2)
    ]
    gain_tile = jnp.concatenate(gain_rows + gain_sums, axis=0)
    gain_tile = jnp.concatenate([gain_tile[0:4], gain_tile[4:8], jnp.zeros((4, 128), F32)], axis=1)
    tile[0] = tile_parts[0] + tile_parts[1] + jnp.concatenate([jnp.zeros((4, 384), F32), gain_tile], axis=0)
    for k in range(1, Z):
        send(tile.at[0], gz.at[k - 1], gz_send.at[k - 1], gz_recv.at[k - 1], z_peers[k - 1])
    for k in range(FAR, 0, -1):
        recv(x_r.at[k - 1], x_send.at[k - 1], x_recv.at[k - 1], xpartner)
        from_sibling(1, k)
        if k == FAR:
            z_s[FAR - 1, 0] = (far(1) + x_r[FAR - 1, 0].astype(F32)).astype(BF16)
            src, dst = z_s.at[FAR - 1, 0], z_r.at[FAR - 1, 0]
        else:
            z_s[k - 1] = (pair(1, k) + x_r[k - 1].astype(F32)).astype(BF16)
            src, dst = z_s.at[k - 1], z_r.at[k - 1]
        send(src, dst, z_send.at[k], z_recv.at[k], (dev(zs(way * k), xl, core), n))
    fin[core] = near(1) + x_r[FAR - 1, 1].astype(F32)
    for j in range(3):
        cols = slice(256 * j, 256 * j + 256)
        left = nf[:, :, cols].reshape(768, 256)
        gu[cols, :] = tn(left, gp[...].reshape(768, 768)).astype(BF16)
        res = tn(left, dqkv[...].reshape(768, 384)).astype(BF16)
        gq[cols, :] = res[:, 0:128]
        gk[cols, :] = res[:, 128:256]
        gv[cols, :] = res[:, 256:384]
    for k in range(1, Z):
        recv(gz.at[k - 1], gz_send.at[k - 1], gz_recv.at[k - 1], z_peers[Z - 1 - k])
    tile[1] = tile[0] + jnp.sum(gz[...], axis=0)
    for j in range(3):
        send(tile.at[1], gquad.at[j], gq_send.at[j], gq_recv.at[j], quad[j])
    for j in range(3):
        recv(gquad.at[j], gq_send.at[j], gq_recv.at[j], quad[j])
    wide_total = tile[1] + gquad[0] + gquad[1] + gquad[2]
    rows[0] = wide_total
    gains[0:4] = wide_total[4:8, 0:128]
    gains[4:8] = wide_total[4:8, 128:256]
    for k, p in enumerate(n_peers):
        send(rows.at[0], rows.at[k + 1], st_send.at[1, k], st_recv.at[1, k], p)
    go[...] = tn(att[...].reshape(768, 128), cf[...].reshape(768, 768)).astype(BF16)

    recv(z_r.at[FAR - 1, 0], z_send.at[FAR], z_recv.at[FAR], (dev(zs(FAR), xl, core), n))
    for k in range(1, FAR):
        recv(z_r.at[k - 1], z_send.at[k], z_recv.at[k], (dev(zs(-way * k), xl, core), n))
    fin[1 - core] = sum(z_r[k, 1 - core].astype(F32) for k in range(FAR - 1))
    fin_s[...] = fin[1 - core].astype(BF16)
    send(fin_s, fin_r, f_sem.at[0], f_sem.at[1], sibling)

    d_own = fin[core] + z_r[FAR - 1, 0].astype(F32) + sum(z_r[k, core].astype(F32) for k in range(FAR - 1))
    ag_wait(gh, every, 3, 2)
    for j in range(3):
        cols = slice(256 * j, 256 * j + 256)
        hidden = gh[:, :, :, :, :, :, cols].reshape(768, 256)
        gd[cols, :] = tn(hidden, cf[...].reshape(768, 768)).astype(BF16)
    recv(fin_r, f_sem.at[0], f_sem.at[1], sibling)
    d_normed = d_own + fin_r[...].astype(F32)
    d_unit = d_normed * ngain
    unit = (x_ref[...].astype(F32) - row_mean) * row_rstd

    for k in range(NARROW - 1):
        recv(rows.at[k + 1], st_send.at[1, k], st_recv.at[1, k], (w, (n - 1 - k + NARROW) % NARROW))
    tile[2] = jnp.sum(rows[...], axis=0)
    own_row = lax.broadcasted_iota(jnp.int32, (24, 384), 0) + (48 * z + 24 * core)
    own_row = own_row == lax.broadcasted_iota(jnp.int32, (24, 384), 1)
    pick_row = lambda i: jnp.sum(jnp.where(own_row, tile[2, pl.ds(2 * xl + i, 1), :], 0.0), axis=1, keepdims=True) / full_width
    first, second = pick_row(0), pick_row(1)
    dx[...] = (cot_ref[...].astype(F32) + row_rstd * (d_unit - first - unit * second)).astype(BF16)

    for c in pending:
        c.wait_send()


def hand_over(*refs):
    srcs, gains_ref, outs, (ngain_ref, qg_ref, kg_ref), sem = refs[:7], refs[7], refs[8:15], refs[15:18], refs[18]
    copies = [pltpu.make_async_copy(s, o, sem.at[i]) for i, (s, o) in enumerate(zip(srcs, outs))]
    for c in copies:
        c.start()
    for i in range(6):
        ngain_ref[pl.ds(128 * i, 128)] = gains_ref[i, :]
    qg_ref[...] = gains_ref[6, :]
    kg_ref[...] = gains_ref[7, :]
    for c in copies:
        c.wait()


def per_device(inputs, cotangent, norm_gain, q_gain, k_gain, w_query, w_key, w_value, w_out, w_up, w_down):
    full_width = inputs.shape[1] * NARROW
    vm = pl.BlockSpec(memory_space=pltpu.VMEM)
    anywhere = pl.BlockSpec(memory_space=pl.ANY)
    v = pltpu.VMEM
    dma = pltpu.SemaphoreType.DMA

    def rs_buffers(c):
        return [
            v((3, 2, 2, 16, c), BF16), v((3, 2, 2, 16, c), BF16), v((3, 2, 16, c), F32),
            v((3, 2, 16, c), BF16), v((3, 2, 16, c), BF16), v((3, 16, c), F32),
            v((3, 16, c), BF16), v((3, 16, c), BF16),
        ]

    grads = [(24, 768), (768, 128), (768, 128), (768, 128), (128, 768), (768, 768), (768, 768)]
    cube = (2, 2, 2, 2, 3, 16)
    scratch = [
        v((768, 1152), BF16), v((896, 768), BF16),
        v((Z, 2, 2, 24, 768), BF16), v((Z, 2, 2, 24, 768), BF16), v((2, 384, 768), BF16), v((2, 384, 768), BF16),
        v((*cube, 896), F32), v((*cube, 384), F32), v((*cube, 768), F32),
        rs_buffers(896), rs_buffers(896), rs_buffers(384), rs_buffers(384), rs_buffers(768), rs_buffers(768),
        v((*cube, 512), BF16), v((*cube, 768), BF16), v((*cube, 768), BF16),
        v((2, 8, 3, 16, 384), BF16), v((2, 8, 3, 16, 128), BF16),
        v((2, Z, 2, 24, 768), F32), v((2, 4, 2, 24, 768), BF16), v((2, 4, 2, 24, 768), BF16),
        v((4, 2, 24, 768), BF16), v((4, 2, 24, 768), BF16), v((4, 2, 24, 768), BF16), v((4, 2, 24, 768), BF16),
        v((2, 24, 768), F32), v((24, 768), BF16), v((24, 768), BF16),
        v((NARROW, 24, 128), F32), v((NARROW, 8, 384), F32),
        v((3, 8, 384), F32), v((3, 8, 384), F32), v((Z - 1, 8, 384), F32),
        dma((6,)), dma((2, 10)), dma((2, 10)), dma((2, 5)), dma((2, 5)), dma((2, 5)), dma((2, 5)),
        dma((6, 3, 3)), dma((6, 3, 3)), dma((4, 3, 3)), dma((4, 3, 3)),
        dma((2, NARROW - 1)), dma((2, NARROW - 1)),
        dma((2, 4)), dma((2, 4)), dma((4,)), dma((4,)), dma((5,)), dma((5,)), dma((2,)), dma((3,)), dma((3,)),
        dma((Z - 1,)), dma((Z - 1,)),
    ]
    grad_shapes = [jax.ShapeDtypeStruct(g, BF16) for g in grads]
    outs = pl.pallas_call(
        functools.partial(kernel, full_width),
        out_shape=(*[v(g, BF16) for g in grads], v((8, 128), F32)),
        in_specs=[vm] * 5 + [pl.BlockSpec(memory_space=pltpu.HBM)] * 6,
        out_specs=[vm] * 8,
        scratch_shapes=scratch,
        compiler_params=pltpu.CompilerParams(
            collective_id=0, has_side_effects=True, vmem_limit_bytes=56 * 1024 * 1024
        ),
        name="layer",
    )(
        inputs, cotangent, norm_gain, q_gain.reshape(1, -1), k_gain.reshape(1, -1),
        w_query, w_key, w_value, w_out, w_up, w_down,
    )
    return pl.pallas_call(
        hand_over,
        out_shape=(
            *grad_shapes,
            jax.ShapeDtypeStruct((768,), F32), jax.ShapeDtypeStruct((128,), F32), jax.ShapeDtypeStruct((128,), F32),
        ),
        in_specs=[vm] * 8,
        out_specs=[anywhere] * 7 + [vm] * 3,
        scratch_shapes=[dma((7,))],
        name="hand_over",
    )(*[pltpu.with_memory_space_constraint(o, pltpu.VMEM) for o in outs])


def solution(mesh):
    return jax.shard_map(
        per_device,
        mesh=mesh,
        in_specs=(
            P("wide", "narrow"), P("wide", "narrow"), P("narrow"), P(), P(),
            P("narrow", "wide"), P("narrow", "wide"), P("narrow", "wide"), P("wide", "narrow"),
            P("narrow", "wide"), P("wide", "narrow"),
        ),
        out_specs=(
            P("wide", "narrow"),
            P("narrow", "wide"), P("narrow", "wide"), P("narrow", "wide"), P("wide", "narrow"),
            P("narrow", "wide"), P("wide", "narrow"),
            P("narrow"), P(), P(),
        ),
        check_vma=False,
    )
```
